128 devices in a mesh: section: 2 (over core), dp: 64 (over z, y, x).
Axes of the slice: x: 4, y: 4, z: 4, core: 2. Of those that a mesh axis runs over, the one named last changes fastest.
Arguments:
- inputs: bfloat16 [128, 128, 4096], P('dp'), may hold values from -6 to 6
- upstream: bfloat16 [128, 128, 4096], P('dp'), may hold values from -6 to 6
- doc_blocks: int32 [128, 2], P('dp'), may hold values from 0 to 1, as said below
- gain: bfloat16 [2, 4096], P('section', 'dp'), may hold values from 0.5 to 1.5
- key_weight: bfloat16 [2, 4096, 512], P('section', 'dp'), may hold values from -0.09375 to 0.09375
- value_weight: bfloat16 [2, 4096, 512], P('section', 'dp'), may hold values from -0.09375 to 0.09375
Outputs:
- grad_inputs: bfloat16 [2, 128, 128, 4096], P('section', 'dp')
- grad_key: float32 [2, 4096, 512], P('section', 'dp')
- grad_value: float32 [2, 4096, 512], P('section', 'dp')
- grad_gain: float32 [2, 4096], P('section', 'dp')
The draws below stay inside these ranges and needn't reach their ends.
Inputs may be any that keep to these rules, and one draw needn't show every extreme that they name: `doc_blocks`: each row starts with document 0, and the number rises by 0 or 1 from one block to the next.
All inputs are finite; a program needn't handle non-finite values.
Results may differ from the reference program's by a relative error of at most 0.02.
Values may be sent and summed in bfloat16 or wider, within the bound.
A program may use at most 192 MiB of HBM per device.

```python
from functools import partial
import jax
import jax.numpy as jnp
from jax import lax

D = 4096
HEAD_DIM = 128
KV_HEADS = 4
BLOCK = 64
BLOCKS = 2
KVW = 512
SEQ = 128
ROWS = 128
LAYERS = 2


def draw_doc_blocks(key, part):
    key = jax.random.fold_in(key, 11)
    starts = jax.random.randint(key, (ROWS, BLOCKS), 0, 2)
    starts = starts.at[0, :].set(1)
    starts = starts.at[:, 0].set(0)
    return jnp.cumsum(starts, axis=1).astype(jnp.int32)


def block_scale(rng, extent, cuts, low, largest):
    def one(axis_at, parts):
        steps = jax.random.uniform(jax.random.fold_in(jax.random.fold_in(rng, 6), axis_at), (parts,), jnp.float32, low / len(cuts), largest / len(cuts))
        return jnp.repeat(jnp.exp(steps), extent[axis_at] // parts).reshape((-1,) + (1,) * (len(extent) - axis_at - 1))

    level = one(*cuts[0])
    for cut in cuts[1:]:
        level = level * one(*cut)
    return level


def gaussian(own_key, shape, scale, most, shards=(), dtype=jnp.bfloat16):
    array = scale * jax.random.normal(own_key, shape, jnp.float32)
    if shards:
        array = array * block_scale(own_key, shape, shards, -0.22, 0.18)
    return jnp.clip(array, -most, most).astype(dtype)


def setup_inputs(seed: int = 0) -> dict:
    key_of = jax.random.split(jax.random.key(seed), 7)
    return {
        "inputs": gaussian(key_of[0], (ROWS, SEQ, D), 1.0, 6.0, ((0, 64),)),
        "upstream": gaussian(key_of[1], (ROWS, SEQ, D), 1.0, 6.0, ((0, 64),)),
        "doc_blocks": draw_doc_blocks(jax.random.fold_in(key_of[6], 71), 0),
        "gain": jnp.clip(1.0 + 0.1 * jax.random.normal(key_of[3], (LAYERS, D), jnp.float32), 0.5, 1.5).astype(jnp.bfloat16),
        "key_weight": gaussian(key_of[4], (LAYERS, D, KVW), D ** -0.5, 0.09375, ((0, 2), (1, 64))),
        "value_weight": gaussian(key_of[5], (LAYERS, D, KVW), D ** -0.5, 0.09375, ((0, 2), (1, 64))),
    }


def normed(activations, gain_values):
    widened = activations.astype(jnp.float32)
    factor = lax.rsqrt(lax.optimization_barrier(jnp.mean(widened * widened, axis=-1, keepdims=True)) + 1e-05)
    return (widened * factor * gain_values).astype(jnp.bfloat16)

def project(hidden, key_weight, value_weight):
    batch_rows, length, model_width = hidden.shape
    flat_rows = hidden.reshape(batch_rows * length, model_width)
    key_rows = jnp.dot(flat_rows, key_weight, preferred_element_type=jnp.float32).astype(jnp.bfloat16)
    value_rows = jnp.dot(flat_rows, value_weight, preferred_element_type=jnp.float32).astype(jnp.bfloat16)
    return (key_rows.reshape(batch_rows, length, -1), value_rows.reshape(batch_rows, length, -1))

def attend(hidden, key_rows, value_rows, documents):
    batch_rows, length, model_width = hidden.shape
    groups = model_width // HEAD_DIM // KV_HEADS
    queries = hidden.reshape(batch_rows, length, KV_HEADS, groups, HEAD_DIM).astype(jnp.float32)
    key_heads = key_rows.reshape(batch_rows, length, KV_HEADS, HEAD_DIM).astype(jnp.float32)
    value_heads = value_rows.reshape(batch_rows, length, KV_HEADS, HEAD_DIM).astype(jnp.float32)
    score_scale = HEAD_DIM ** (-0.5)
    key_docs = jnp.repeat(documents, BLOCK, axis=1)
    pieces = []
    for block_index in range(length // BLOCK):
        query_block = queries[:, block_index * BLOCK:(block_index + 1) * BLOCK]
        scores = jnp.einsum('bqhgd,bkhd->bhgqk', query_block, key_heads) * score_scale
        same_doc = key_docs == documents[:, block_index:block_index + 1]
        query_pos = block_index * BLOCK + jnp.arange(BLOCK)
        causal = jnp.arange(length)[None, :] <= query_pos[:, None]
        allowed = same_doc[:, None, None, None, :] & causal[None, None, None, :, :]
        scores = jnp.where(allowed, scores, -1e+30)
        weights = jnp.exp(scores)
        probability = (weights / lax.optimization_barrier(jnp.sum(weights, axis=-1, keepdims=True))).astype(jnp.bfloat16)
        mixture = jnp.einsum('bhgqk,bkhd->bqhgd', probability.astype(jnp.float32), value_heads)
        pieces.append(mixture.reshape(batch_rows, BLOCK, model_width))
    return jnp.concatenate(pieces, axis=1)

def layer_forward(activations, gain_values, key_weight, value_weight, documents):
    hidden = normed(activations, gain_values)
    key_rows, value_rows = project(hidden, key_weight, value_weight)
    return (activations.astype(jnp.float32) + attend(hidden, key_rows, value_rows, documents)).astype(jnp.bfloat16)

def layer_backward(activations, cotangent, gain_values, key_weight, value_weight, documents):
    hidden, norm_back = jax.vjp(normed, activations, gain_values)
    key_rows, value_rows = project(hidden, key_weight, value_weight)
    core_out, core_back = jax.vjp(partial(attend, documents=documents), hidden, key_rows, value_rows)
    query_grad, key_grad, value_grad = core_back(cotangent.astype(jnp.float32))
    key_flat = key_grad.reshape(-1, key_weight.shape[1])
    value_flat = value_grad.reshape(-1, value_weight.shape[1])
    through = jnp.dot(key_flat, key_weight.T, preferred_element_type=jnp.float32) + jnp.dot(value_flat, value_weight.T, preferred_element_type=jnp.float32)
    hidden_grad = (query_grad.astype(jnp.float32) + through.reshape(hidden.shape)).astype(jnp.bfloat16)
    input_grad, gain_grad = norm_back(hidden_grad)
    total = (cotangent.astype(jnp.float32) + input_grad.astype(jnp.float32)).astype(jnp.bfloat16)
    return (total, gain_grad, hidden, key_grad, value_grad)

def reference(inputs, upstream, doc_blocks, gain, key_weight, value_weight):
    layer_count = gain.shape[0]
    gain_values = gain.astype(jnp.float32)
    model_width = inputs.shape[2]
    key_width = key_weight.shape[2]

    def one_row(totals, row_data):
        activations, cotangent, documents = row_data
        current = activations[None]
        row_docs = documents[None]
        saved = []
        for layer_index in range(layer_count):
            saved.append(current)
            current = layer_forward(current, gain_values[layer_index], key_weight[layer_index], value_weight[layer_index], row_docs)
        total_key, total_value, total_gain = totals
        flowing = cotangent[None]
        input_grads = [None] * layer_count
        for layer_index in reversed(range(layer_count)):
            flowing, gain_grad, hidden, key_grad, value_grad = layer_backward(saved[layer_index], flowing, gain_values[layer_index], key_weight[layer_index], value_weight[layer_index], row_docs)
            input_grads[layer_index] = flowing[0]
            hidden_flat = hidden.reshape(-1, model_width)
            total_key = total_key.at[layer_index].add(jnp.dot(hidden_flat.T, key_grad.reshape(-1, key_width), preferred_element_type=jnp.float32))
            total_value = total_value.at[layer_index].add(jnp.dot(hidden_flat.T, value_grad.reshape(-1, key_width), preferred_element_type=jnp.float32))
            total_gain = total_gain.at[layer_index].add(gain_grad)
        return ((total_key, total_value, total_gain), jnp.stack(input_grads))
    start_totals = (jnp.zeros((layer_count, model_width, key_width), jnp.float32), jnp.zeros((layer_count, model_width, key_width), jnp.float32), jnp.zeros((layer_count, model_width), jnp.float32))
    totals, per_row = lax.scan(one_row, start_totals, (inputs, upstream, doc_blocks))
    return (jnp.transpose(per_row, (1, 0, 2, 3)), totals[0], totals[1], totals[2])
```

```python
import functools
from functools import partial

import jax
import jax.numpy as jnp
from jax import lax
from jax.experimental import pallas as pl
from jax.experimental.pallas import tpu as pltpu
from jax.sharding import PartitionSpec as P

HEAD_DIM = 128
KV_HEADS = 4
BLOCK = 64
STRIDE = {"x": 1, "y": 4, "z": 16}
COLOURS = ((("x", "y", "z"), 0, 384), (("z", "y", "x"), 384, 384), (("x", "z", "y"), 768, 256))
ROWS = 64
MESH = pl.DeviceIdType.MESH


class Torus:
    def __init__(self):
        self.section = lax.axis_index("section")
        self.me = lax.axis_index("dp")
        self.pos = {
            "x": lax.rem(self.me, 4),
            "y": lax.rem(self.me // 4, 4),
            "z": self.me // 16,
        }

    def at(self, axis, delta):
        return lax.rem(self.pos[axis] + delta, 4)

    def peer(self, axis, delta):
        return (self.section, self.me + (self.at(axis, delta) - self.pos[axis]) * STRIDE[axis])

    def barrier(self):
        sem = pltpu.get_barrier_semaphore()
        for axis in "xyz":
            for delta in (1, 2, 3):
                pl.semaphore_signal(sem, inc=1, device_id=self.peer(axis, delta), device_id_type=MESH)
        pl.semaphore_wait(sem, 9)


def remote(src, dst, sems, index, device):
    return pltpu.make_async_remote_copy(
        src_ref=src, dst_ref=dst, send_sem=sems[0].at[index], recv_sem=sems[1].at[index],
        device_id=device, device_id_type=MESH)


def block(buf, torus, axes, phase, index):
    first, mid, last = axes
    if phase == 2:
        return buf.at[index]
    if phase == 1:
        return buf.at[torus.pos[last], index]
    return buf.at[torus.pos[last], torus.pos[mid], index]


def half(ref, which):
    size = ref.shape[0] // 2
    return ref.at[pl.ds(which * size, size)]


def gather_phase(torus, bufs, sems, phase):
    sends = []

    def send(c, k, ref, axis, delta):
        copy = remote(ref, ref, sems, (c, phase, k), torus.peer(axis, delta))
        copy.start()
        sends.append(copy)

    def arrived(c, k, ref, axis):
        remote(ref, ref, sems, (c, phase, k), torus.peer(axis, 1)).wait_recv()

    for c, (axes, _, _) in enumerate(COLOURS):
        axis = axes[phase]
        own = block(bufs[c], torus, axes, phase, torus.pos[axis])
        send(c, 0, half(own, 0), axis, 1)
        send(c, 2, half(own, 1), axis, 3)
        send(c, 1, half(own, 1), axis, 1)
        send(c, 3, half(own, 0), axis, 3)
    for c, (axes, _, _) in enumerate(COLOURS):
        axis = axes[phase]
        before = block(bufs[c], torus, axes, phase, torus.at(axis, 3))
        after = block(bufs[c], torus, axes, phase, torus.at(axis, 1))
        arrived(c, 0, half(before, 0), axis)
        send(c, 4, half(before, 0), axis, 1)
        arrived(c, 2, half(after, 1), axis)
        send(c, 5, half(after, 1), axis, 3)
    for c, (axes, _, _) in enumerate(COLOURS):
        axis = axes[phase]
        before = block(bufs[c], torus, axes, phase, torus.at(axis, 3))
        after = block(bufs[c], torus, axes, phase, torus.at(axis, 1))
        far = block(bufs[c], torus, axes, phase, torus.at(axis, 2))
        arrived(c, 1, half(before, 1), axis)
        arrived(c, 3, half(after, 0), axis)
        arrived(c, 4, half(far, 0), axis)
        arrived(c, 5, half(far, 1), axis)
    return sends


def gain_phase(torus, buf, sems, phase):
    axis = "xyz"[phase]
    axes = ("x", "y", "z")
    own = block(buf, torus, axes, phase, torus.pos[axis])
    sends = []
    for delta in (1, 2, 3):
        copy = remote(own, own, sems, (phase, delta - 1), torus.peer(axis, delta))
        copy.start()
        sends.append(copy)
    for delta in (1, 2, 3):
        other = block(buf, torus, axes, phase, torus.at(axis, 4 - delta))
        remote(other, other, sems, (phase, delta - 1), torus.peer(axis, delta)).wait_recv()
    return sends


def gather_kernel(gain_ref, key_ref, value_ref, g0, g1, g2, gg, local_sem, send_sem, recv_sem, gsend_sem, grecv_sem):
    torus = Torus()
    bufs = (g0, g1, g2)

    def slot(c):
        axes = COLOURS[c][0]
        return block(bufs[c], torus, axes, 0, torus.pos[axes[0]])

    local = [
        pltpu.make_async_copy(key_ref.at[:, pl.ds(0, 384)], slot(0), local_sem.at[0]),
        pltpu.make_async_copy(key_ref.at[:, pl.ds(384, 128)], slot(1).at[:, pl.ds(0, 128)], local_sem.at[1]),
        pltpu.make_async_copy(value_ref.at[:, pl.ds(0, 256)], slot(1).at[:, pl.ds(128, 256)], local_sem.at[2]),
        pltpu.make_async_copy(value_ref.at[:, pl.ds(256, 256)], slot(2), local_sem.at[3]),
        pltpu.make_async_copy(gain_ref, gg.at[torus.pos["z"], torus.pos["y"], torus.pos["x"]], local_sem.at[4]),
    ]
    for copy in local:
        copy.start()
    torus.barrier()
    for copy in local:
        copy.wait()
    sends = []
    for phase in range(3):
        sends += gain_phase(torus, gg, (gsend_sem, grecv_sem), phase)
        sends += gather_phase(torus, bufs, (send_sem, recv_sem), phase)
    for copy in sends:
        copy.wait_send()


def gathered(gain_slab, key_weight, value_weight):
    vmem = pl.BlockSpec(memory_space=pltpu.VMEM)
    return pl.pallas_call(
        gather_kernel,
        out_shape=[jax.ShapeDtypeStruct((4, 4, 4, ROWS, w), jnp.bfloat16) for _, _, w in COLOURS]
        + [jax.ShapeDtypeStruct((4, 4, 4, 8, 128), jnp.float32)],
        in_specs=[vmem] * 3,
        out_specs=[vmem] * 4,
        scratch_shapes=[
            pltpu.SemaphoreType.DMA((5,)),
            pltpu.SemaphoreType.DMA((3, 3, 6)),
            pltpu.SemaphoreType.DMA((3, 3, 6)),
            pltpu.SemaphoreType.DMA((3, 3)),
            pltpu.SemaphoreType.DMA((3, 3)),
        ],
        compiler_params=pltpu.CompilerParams(
            collective_id=0, has_side_effects=True, vmem_limit_bytes=48 * 1024 * 1024),
        name="gather",
    )(gain_slab, key_weight, value_weight)


def add_into(dst, *others):
    lead = dst.shape[:-2]
    count = 1
    for n in lead:
        count *= n

    def body(i, carry):
        index = []
        rest = i
        for n in reversed(lead):
            index.insert(0, lax.rem(rest, n))
            rest = rest // n
        index = tuple(index)
        total = dst[index].astype(jnp.float32)
        for other in others:
            total = total + other[index].astype(jnp.float32)
        dst[index] = total.astype(dst.dtype)
        return carry

    if count == 1 and not lead:
        total = dst[...].astype(jnp.float32)
        for other in others:
            total = total + other[...].astype(jnp.float32)
        dst[...] = total.astype(dst.dtype)
    else:
        lax.fori_loop(0, count, body, 0)


def scatter_phase(torus, bufs, inbox, sems, phase):
    sends = []

    def send(c, k, ref, axis, delta):
        copy = remote(ref, inbox[c].at[k], sems, (c, phase, k), torus.peer(axis, delta))
        copy.start()
        sends.append(copy)

    def arrived(c, k, axis):
        slot = inbox[c].at[k]
        remote(slot, slot, sems, (c, phase, k), torus.peer(axis, 1)).wait_recv()

    for c, (axes, _, _) in enumerate(COLOURS):
        axis = axes[phase]
        far = block(bufs[c], torus, axes, phase, torus.at(axis, 2))
        after = block(bufs[c], torus, axes, phase, torus.at(axis, 1))
        before = block(bufs[c], torus, axes, phase, torus.at(axis, 3))
        send(c, 0, half(far, 0), axis, 1)
        send(c, 1, half(far, 1), axis, 3)
        send(c, 2, half(after, 1), axis, 1)
        send(c, 3, half(before, 0), axis, 3)
    for c, (axes, _, _) in enumerate(COLOURS):
        axis = axes[phase]
        after = block(bufs[c], torus, axes, phase, torus.at(axis, 1))
        before = block(bufs[c], torus, axes, phase, torus.at(axis, 3))
        arrived(c, 0, axis)
        add_into(half(after, 0), inbox[c].at[0])
        send(c, 4, half(after, 0), axis, 1)
        arrived(c, 1, axis)
        add_into(half(before, 1), inbox[c].at[1])
        send(c, 5, half(before, 1), axis, 3)
    for c, (axes, _, _) in enumerate(COLOURS):
        axis = axes[phase]
        own = block(bufs[c], torus, axes, phase, torus.pos[axis])
        arrived(c, 3, axis)
        arrived(c, 4, axis)
        add_into(half(own, 0), inbox[c].at[3], inbox[c].at[4])
        arrived(c, 2, axis)
        arrived(c, 5, axis)
        add_into(half(own, 1), inbox[c].at[2], inbox[c].at[5])
    return sends


def gain_scatter_phase(torus, buf, inbox, sems, phase):
    axis = "xyz"[phase]
    axes = ("x", "y", "z")
    sends = []
    for delta in (1, 2, 3):
        other = block(buf, torus, axes, phase, torus.at(axis, delta))
        copy = remote(other, inbox.at[delta - 1], sems, (phase, delta - 1), torus.peer(axis, delta))
        copy.start()
        sends.append(copy)
    own = block(buf, torus, axes, phase, torus.pos[axis])
    for delta in (1, 2, 3):
        slot = inbox.at[delta - 1]
        remote(slot, slot, sems, (phase, delta - 1), torus.peer(axis, delta)).wait_recv()
    add_into(own, inbox.at[0], inbox.at[1], inbox.at[2])
    return sends


def scatter_kernel(s0, s1, s2, sg, key_ref, value_ref, gain_ref, b0, b1, b2, bg, r20, r21, r22, r10, r11, r12, r00, r01, r02,
                   q2, q1, q0, local_sem, send_sem, recv_sem, gsend_sem, grecv_sem):
    torus = Torus()
    bufs = (b0, b1, b2)
    local = [
        pltpu.make_async_copy(src, dst, local_sem.at[i])
        for i, (src, dst) in enumerate(((s0, b0), (s1, b1), (s2, b2), (sg, bg)))
    ]
    for copy in local:
        copy.start()
    torus.barrier()
    for copy in local:
        copy.wait()
    sends = []
    inboxes = {2: (r20, r21, r22), 1: (r10, r11, r12), 0: (r00, r01, r02)}
    quick = {2: q2, 1: q1, 0: q0}
    for phase in (2, 1, 0):
        sends += gain_scatter_phase(torus, bg, quick[phase], (gsend_sem, grecv_sem), phase)
        sends += scatter_phase(torus, bufs, inboxes[phase], (send_sem, recv_sem), phase)
    for copy in sends:
        copy.wait_send()

    def mine(c):
        axes = COLOURS[c][0]
        return block(bufs[c], torus, axes, 0, torus.pos[axes[0]])[...].astype(jnp.float32)

    m1 = mine(1)
    key_ref[:, 0:384] = mine(0)
    key_ref[:, 384:512] = m1[:, 0:128]
    value_ref[:, 0:256] = m1[:, 128:384]
    value_ref[:, 256:512] = mine(2)
    gain_ref[...] = bg[torus.pos["z"], torus.pos["y"], torus.pos["x"]]


def scattered(parts, gain_part):
    vmem = pl.BlockSpec(memory_space=pltpu.VMEM)
    anywhere = pl.BlockSpec(memory_space=pl.ANY)
    return pl.pallas_call(
        scatter_kernel,
        out_shape=[jax.ShapeDtypeStruct((ROWS, 512), jnp.float32)] * 2 + [jax.ShapeDtypeStruct((8, 128), jnp.float32)],
        in_specs=[anywhere] * 4,
        out_specs=[vmem] * 3,
        scratch_shapes=[pltpu.VMEM((4, 4, 4, ROWS, w), jnp.bfloat16) for _, _, w in COLOURS]
        + [pltpu.VMEM((4, 4, 4, 8, 128), jnp.float32)]
        + [pltpu.VMEM((6, 2, 4, ROWS, w), jnp.bfloat16) for _, _, w in COLOURS]
        + [pltpu.VMEM((6, 2, ROWS, w), jnp.bfloat16) for _, _, w in COLOURS]
        + [pltpu.VMEM((6, ROWS // 2, w), jnp.bfloat16) for _, _, w in COLOURS]
        + [pltpu.VMEM((3, 4, 4, 8, 128), jnp.float32), pltpu.VMEM((3, 4, 8, 128), jnp.float32), pltpu.VMEM((3, 8, 128), jnp.float32)]
        + [
            pltpu.SemaphoreType.DMA((4,)),
            pltpu.SemaphoreType.DMA((3, 3, 6)),
            pltpu.SemaphoreType.DMA((3, 3, 6)),
            pltpu.SemaphoreType.DMA((3, 3)),
            pltpu.SemaphoreType.DMA((3, 3)),
        ],
        compiler_params=pltpu.CompilerParams(
            collective_id=1, has_side_effects=True, vmem_limit_bytes=48 * 1024 * 1024),
        name="scatter",
    )(*parts, gain_part)


def whole(parts):
    out = []
    for (axes, _, w), part in zip(COLOURS, parts):
        order = [2 - axes.index(a) for a in "zyx"]
        out.append(jnp.transpose(part, order + [3, 4]).reshape(4096, w))
    return jnp.concatenate(out, axis=1)


def parted(full):
    out = []
    for axes, start, w in COLOURS:
        piece = full[:, start:start + w].reshape(4, 4, 4, ROWS, w)
        order = ["zyx".index(a) for a in reversed(axes)]
        out.append(jnp.transpose(piece, order + [3, 4]))
    return out


def from_behind(x, axis, by):
    peers = lax.axis_size(axis)
    pairs = [(i, i + by) for i in range(peers) if 0 <= i + by < peers]
    return lax.ppermute(x, axis, pairs)


def normed(activations, gain_values):
    widened = activations.astype(jnp.float32)
    factor = lax.rsqrt(jnp.mean(widened * widened, axis=-1, keepdims=True) + 1e-05)
    return (widened * factor * gain_values).astype(jnp.bfloat16)


def project(hidden, key_weight, value_weight):
    batch_rows, length, model_width = hidden.shape
    flat_rows = hidden.reshape(batch_rows * length, model_width)
    key_rows = jnp.dot(flat_rows, key_weight, preferred_element_type=jnp.float32).astype(
        jnp.bfloat16
    )
    value_rows = jnp.dot(flat_rows, value_weight, preferred_element_type=jnp.float32).astype(
        jnp.bfloat16
    )
    return (key_rows.reshape(batch_rows, length, -1), value_rows.reshape(batch_rows, length, -1))


def attend(hidden, key_rows, value_rows, documents):
    batch_rows, length, model_width = hidden.shape
    groups = model_width // HEAD_DIM // KV_HEADS
    queries = hidden.reshape(batch_rows, length, KV_HEADS, groups, HEAD_DIM)
    key_heads = key_rows.reshape(batch_rows, length, KV_HEADS, HEAD_DIM)
    value_heads = value_rows.reshape(batch_rows, length, KV_HEADS, HEAD_DIM)
    score_scale = HEAD_DIM ** (-0.5)
    key_docs = jnp.repeat(documents, BLOCK, axis=1)
    pieces = []
    for block_index in range(length // BLOCK):
        query_block = queries[:, block_index * BLOCK : (block_index + 1) * BLOCK]
        scores = (
            jnp.einsum(
                "bqhgd,bkhd->bhgqk", query_block, key_heads, preferred_element_type=jnp.float32
            )
            * score_scale
        )
        same_doc = key_docs == documents[:, block_index : block_index + 1]
        query_pos = block_index * BLOCK + jnp.arange(BLOCK)
        causal = jnp.arange(length)[None, :] <= query_pos[:, None]
        allowed = same_doc[:, None, None, None, :] & causal[None, None, None, :, :]
        scores = jnp.where(allowed, scores, -1e30)
        weights = jnp.exp(scores)
        probability = (weights / jnp.sum(weights, axis=-1, keepdims=True)).astype(jnp.bfloat16)
        mixture = jnp.einsum(
            "bhgqk,bkhd->bqhgd", probability, value_heads, preferred_element_type=jnp.float32
        )
        pieces.append(mixture.reshape(batch_rows, BLOCK, model_width))
    return jnp.concatenate(pieces, axis=1)


def layer_forward(activations, gain_values, key_weight, value_weight, documents):
    hidden = normed(activations, gain_values)
    key_rows, value_rows = project(hidden, key_weight, value_weight)
    return (
        activations.astype(jnp.float32) + attend(hidden, key_rows, value_rows, documents)
    ).astype(jnp.bfloat16)


def layer_backward(activations, cotangent, gain_values, key_weight, value_weight, documents):
    hidden, norm_back = jax.vjp(normed, activations, gain_values)
    key_rows, value_rows = project(hidden, key_weight, value_weight)
    core_out, core_back = jax.vjp(
        partial(attend, documents=documents), hidden, key_rows, value_rows
    )
    query_grad, key_grad, value_grad = core_back(cotangent.astype(jnp.float32))
    key_flat = key_grad.reshape(-1, key_weight.shape[1])
    value_flat = value_grad.reshape(-1, value_weight.shape[1])
    through = jnp.dot(key_flat, key_weight.T, preferred_element_type=jnp.float32) + jnp.dot(
        value_flat, value_weight.T, preferred_element_type=jnp.float32
    )
    hidden_grad = (query_grad.astype(jnp.float32) + through.reshape(hidden.shape)).astype(
        jnp.bfloat16
    )
    input_grad, gain_grad = norm_back(hidden_grad)
    total = (cotangent.astype(jnp.float32) + input_grad.astype(jnp.float32)).astype(jnp.bfloat16)
    return (total, gain_grad, hidden, key_grad, value_grad)


def shards(inputs, upstream, doc_blocks, gain, key_weight, value_weight):
    section = lax.axis_index("section")
    odd = lax.rem(lax.axis_index("dp"), 2) == 1
    row = gain[0].astype(jnp.float32)
    still = jnp.zeros_like(row)
    lane = jnp.where(odd, jnp.concatenate([still, row]), jnp.concatenate([row, still]))
    slab = jnp.broadcast_to(lane[None], (8, 128))
    *parts, gains = gathered(slab, key_weight[0], value_weight[0])
    weights = whole(parts)
    key_whole, value_whole = weights[:, :512], weights[:, 512:]
    pairs = gains[:, :, :, 0].reshape(32, 2, 128)
    gain_values = (pairs[:, 0] + pairs[:, 1]).reshape(4096)
    result = layer_forward(inputs, gain_values, key_whole, value_whole, doc_blocks)
    arrived = from_behind(result, "section", 1)
    entering = jnp.where(section == 0, inputs, arrived)
    first = layer_backward(entering, upstream, gain_values, key_whole, value_whole, doc_blocks)
    back = from_behind(first[0], "section", -1)
    cotangent = jnp.where(section == 0, back, upstream)
    second = layer_backward(entering, cotangent, gain_values, key_whole, value_whole, doc_blocks)
    total, gain_grad, hidden, key_grad, value_grad = second
    grads = jnp.concatenate([key_grad.reshape(256, 512), value_grad.reshape(256, 512)], axis=1)
    full = jnp.dot(hidden.reshape(256, 4096).T, grads, preferred_element_type=jnp.float32).astype(jnp.bfloat16)
    gg = gain_grad.reshape(64, 64)
    z = jnp.zeros_like(gg)
    par = (jnp.arange(64) % 2 == 1)[:, None]
    gg = jnp.where(par, jnp.concatenate([z, gg], 1), jnp.concatenate([gg, z], 1))
    gg = jnp.broadcast_to(gg[:, None], (64, 8, 128)).reshape(4, 4, 4, 8, 128)
    key_share, value_share, gain_share = scattered(parted(full), gg)
    gain_share = jnp.where(odd, gain_share[0, 64:], gain_share[0, :64])
    return (total[None], key_share[None], value_share[None], gain_share[None])


def solution(mesh):
    in_specs = (
        P("dp", None, None),
        P("dp", None, None),
        P("dp", None),
        P("section", "dp"),
        P("section", "dp", None),
        P("section", "dp", None),
    )
    out_specs = (
        P("section", "dp", None, None),
        P("section", "dp", None),
        P("section", "dp", None),
        P("section", "dp"),
    )
    return jax.shard_map(shards, mesh=mesh, in_specs=in_specs, out_specs=out_specs, check_vma=False)
```

```python
import jax
import jax.numpy as jnp
from jax import lax
from jax.experimental import pallas as pl
from jax.experimental.pallas import tpu as pltpu
from jax.sharding import PartitionSpec as P

HEAD_DIM = 128
KV_HEADS = 4
BLOCK = 64
STRIDE = {"x": 1, "y": 4, "z": 16}
COLOURS = ((("x", "y", "z"), 0, 384), (("z", "y", "x"), 384, 384), (("x", "z", "y"), 768, 256))
ROWS = 64
MESH = pl.DeviceIdType.MESH


class Torus:
    def __init__(self):
        self.section = lax.axis_index("section")
        self.me = lax.axis_index("dp")
        self.pos = {
            "x": lax.rem(self.me, 4),
            "y": lax.rem(self.me // 4, 4),
            "z": self.me // 16,
        }

    def at(self, axis, delta):
        return lax.rem(self.pos[axis] + delta, 4)

    def peer(self, axis, delta):
        return (self.section, self.me + (self.at(axis, delta) - self.pos[axis]) * STRIDE[axis])

    def barrier(self):
        sem = pltpu.get_barrier_semaphore()
        for axis in "xyz":
            for delta in (1, 2, 3):
                pl.semaphore_signal(sem, inc=1, device_id=self.peer(axis, delta), device_id_type=MESH)
        pl.semaphore_signal(sem, inc=1, device_id=self.other(), device_id_type=MESH)
        pl.semaphore_wait(sem, 10)

    def other(self):
        return (1 - self.section, self.me)


def remote(src, dst, sems, index, device):
    return pltpu.make_async_remote_copy(
        src_ref=src, dst_ref=dst, send_sem=sems[0].at[index], recv_sem=sems[1].at[index],
        device_id=device, device_id_type=MESH)


def block(buf, torus, axes, phase, index):
    first, mid, last = axes
    if phase == 2:
        return buf.at[index]
    if phase == 1:
        return buf.at[torus.pos[last], index]
    return buf.at[torus.pos[last], torus.pos[mid], index]


def half(ref, which):
    size = ref.shape[0] // 2
    return ref.at[pl.ds(which * size, size)]


def gather_phase(torus, bufs, sems, phase):
    sends = []

    def send(c, k, ref, axis, delta):
        copy = remote(ref, ref, sems, (c, phase, k), torus.peer(axis, delta))
        copy.start()
        sends.append(copy)

    def arrived(c, k, ref, axis):
        remote(ref, ref, sems, (c, phase, k), torus.peer(axis, 1)).wait_recv()

    for c, (axes, _, _) in enumerate(COLOURS):
        axis = axes[phase]
        own = block(bufs[c], torus, axes, phase, torus.pos[axis])
        send(c, 0, half(own, 0), axis, 1)
        send(c, 2, half(own, 1), axis, 3)
        send(c, 1, half(own, 1), axis, 1)
        send(c, 3, half(own, 0), axis, 3)
    for c, (axes, _, _) in enumerate(COLOURS):
        axis = axes[phase]
        before = block(bufs[c], torus, axes, phase, torus.at(axis, 3))
        after = block(bufs[c], torus, axes, phase, torus.at(axis, 1))
        arrived(c, 0, half(before, 0), axis)
        send(c, 4, half(before, 0), axis, 1)
        arrived(c, 2, half(after, 1), axis)
        send(c, 5, half(after, 1), axis, 3)
    for c, (axes, _, _) in enumerate(COLOURS):
        axis = axes[phase]
        before = block(bufs[c], torus, axes, phase, torus.at(axis, 3))
        after = block(bufs[c], torus, axes, phase, torus.at(axis, 1))
        far = block(bufs[c], torus, axes, phase, torus.at(axis, 2))
        arrived(c, 1, half(before, 1), axis)
        arrived(c, 3, half(after, 0), axis)
        arrived(c, 4, half(far, 0), axis)
        arrived(c, 5, half(far, 1), axis)
    return sends


def gain_phase(torus, buf, sems, phase):
    axis = "xyz"[phase]
    axes = ("x", "y", "z")
    own = block(buf, torus, axes, phase, torus.pos[axis])
    sends = []
    for delta in (1, 2, 3):
        copy = remote(own, own, sems, (phase, delta - 1), torus.peer(axis, delta))
        copy.start()
        sends.append(copy)
    for delta in (1, 2, 3):
        other = block(buf, torus, axes, phase, torus.at(axis, 4 - delta))
        remote(other, other, sems, (phase, delta - 1), torus.peer(axis, delta)).wait_recv()
    return sends


def add_into(dst, *others):
    lead = dst.shape[:-2]
    count = 1
    for n in lead:
        count *= n

    def body(i, carry):
        index = []
        rest = i
        for n in reversed(lead):
            index.insert(0, lax.rem(rest, n))
            rest = rest // n
        index = tuple(index)
        total = dst[index].astype(jnp.float32)
        for other in others:
            total = total + other[index].astype(jnp.float32)
        dst[index] = total.astype(dst.dtype)
        return carry

    if count == 1 and not lead:
        total = dst[...].astype(jnp.float32)
        for other in others:
            total = total + other[...].astype(jnp.float32)
        dst[...] = total.astype(dst.dtype)
    else:
        lax.fori_loop(0, count, body, 0)


def scatter_phase(torus, bufs, inbox, sems, phase):
    sends = []

    def send(c, k, ref, axis, delta):
        copy = remote(ref, inbox[c].at[k], sems, (c, phase, k), torus.peer(axis, delta))
        copy.start()
        sends.append(copy)

    def arrived(c, k, axis):
        slot = inbox[c].at[k]
        remote(slot, slot, sems, (c, phase, k), torus.peer(axis, 1)).wait_recv()

    for c, (axes, _, _) in enumerate(COLOURS):
        axis = axes[phase]
        far = block(bufs[c], torus, axes, phase, torus.at(axis, 2))
        after = block(bufs[c], torus, axes, phase, torus.at(axis, 1))
        before = block(bufs[c], torus, axes, phase, torus.at(axis, 3))
        send(c, 0, half(far, 0), axis, 1)
        send(c, 1, half(far, 1), axis, 3)
        send(c, 2, half(after, 1), axis, 1)
        send(c, 3, half(before, 0), axis, 3)
    for c, (axes, _, _) in enumerate(COLOURS):
        axis = axes[phase]
        after = block(bufs[c], torus, axes, phase, torus.at(axis, 1))
        before = block(bufs[c], torus, axes, phase, torus.at(axis, 3))
        arrived(c, 0, axis)
        add_into(half(after, 0), inbox[c].at[0])
        send(c, 4, half(after, 0), axis, 1)
        arrived(c, 1, axis)
        add_into(half(before, 1), inbox[c].at[1])
        send(c, 5, half(before, 1), axis, 3)
    for c, (axes, _, _) in enumerate(COLOURS):
        axis = axes[phase]
        own = block(bufs[c], torus, axes, phase, torus.pos[axis])
        arrived(c, 3, axis)
        arrived(c, 4, axis)
        add_into(half(own, 0), inbox[c].at[3], inbox[c].at[4])
        arrived(c, 2, axis)
        arrived(c, 5, axis)
        add_into(half(own, 1), inbox[c].at[2], inbox[c].at[5])
    return sends


def gain_scatter_phase(torus, buf, inbox, sems, phase):
    axis = "xyz"[phase]
    axes = ("x", "y", "z")
    sends = []
    for delta in (1, 2, 3):
        other = block(buf, torus, axes, phase, torus.at(axis, delta))
        copy = remote(other, inbox.at[delta - 1], sems, (phase, delta - 1), torus.peer(axis, delta))
        copy.start()
        sends.append(copy)
    own = block(buf, torus, axes, phase, torus.pos[axis])
    for delta in (1, 2, 3):
        slot = inbox.at[delta - 1]
        remote(slot, slot, sems, (phase, delta - 1), torus.peer(axis, delta)).wait_recv()
    add_into(own, inbox.at[0], inbox.at[1], inbox.at[2])
    return sends


def chunk_of(bufs, c, z, y):
    index = {"z": z, "y": y, "x": slice(None)}
    first, mid, last = COLOURS[c][0]
    return bufs[c].at[index[last], index[mid], index[first]]


def dot(a, b):
    return jnp.dot(a, b, preferred_element_type=jnp.float32)


def dot_nt(a, b):
    return lax.dot_general(a, b, (((1,), (1,)), ((), ())), preferred_element_type=jnp.float32)


def rows(i, size):
    return pl.ds(pl.multiple_of(i * size, size), size)


def layer_kernel(
    bias_ref, gain_ref, key_ref, value_ref, inputs_ref, upstream_ref,
    out_ref, key_out, value_out, gain_out,
    g0, g1, g2, gg, b0, b1, b2, bg, r20, r21, r22, r10, r11, r12, r00, r01, r02, q2, q1, q0,
    nat, x_t, out_t, h_t, h_nat, c_t, dh_t, p_t, kv, kv_t, dkv, dkv_t, gcol, ggcol, acc, stat,
    local_sem, send_sem, recv_sem, gsend_sem, grecv_sem, ssend_sem, srecv_sem, sgsend_sem, sgrecv_sem, cross_send, cross_recv,
):
    torus = Torus()
    section = torus.section
    bufs, sums = (g0, g1, g2), (b0, b1, b2)
    first_core, second_core = section == 0, section == 1

    def slot(c):
        axes = COLOURS[c][0]
        return block(bufs[c], torus, axes, 0, torus.pos[axes[0]])

    local = [
        pltpu.make_async_copy(key_ref.at[:, pl.ds(0, 384)], slot(0), local_sem.at[0]),
        pltpu.make_async_copy(key_ref.at[:, pl.ds(384, 128)], slot(1).at[:, pl.ds(0, 128)], local_sem.at[1]),
        pltpu.make_async_copy(value_ref.at[:, pl.ds(0, 256)], slot(1).at[:, pl.ds(128, 256)], local_sem.at[2]),
        pltpu.make_async_copy(value_ref.at[:, pl.ds(256, 256)], slot(2), local_sem.at[3]),
        pltpu.make_async_copy(gain_ref, gg.at[torus.pos["z"], torus.pos["y"], torus.pos["x"]], local_sem.at[4]),
    ]
    for copy in local:
        copy.start()
    load_inputs = pltpu.make_async_copy(inputs_ref, nat, local_sem.at[5])
    load_upstream = pltpu.make_async_copy(upstream_ref, nat, local_sem.at[6])
    pl.when(first_core)(load_inputs.start)
    pl.when(second_core)(load_upstream.start)
    torus.barrier()
    for copy in local:
        copy.wait()
    pl.when(first_core)(load_inputs.wait)
    pl.when(second_core)(load_upstream.wait)

    sends = []
    for phase in range(3):
        sends += gain_phase(torus, gg, (gsend_sem, grecv_sem), phase)
        sends += gather_phase(torus, bufs, (send_sem, recv_sem), phase)

    def turn(src, dst):
        def body(i, carry):
            dst[rows(i, 512), :] = src[:, rows(i, 512)].T
            return carry

        lax.fori_loop(0, 8, body, 0)

    def square_sums(start, count):
        def body(i, carry):
            x = x_t[rows(start + i, 128), :].astype(jnp.float32)
            return carry + jnp.sum((x * x).reshape(16, 8, 256), axis=0)

        return lax.fori_loop(0, count, body, jnp.zeros((8, 256), jnp.float32))

    ggcol[...] = jnp.zeros_like(ggcol)
    for j in range(32):
        i = 2 * j
        one = gg[i // 16, i // 4 % 4, i % 4]
        two = gg[i // 16, i // 4 % 4, i % 4 + 1]
        ggcol[j:j + 1, :] = (one + two)[0:1]
    gcol[...] = ggcol[...].T
    lane = lax.broadcasted_iota(jnp.int32, (128, 128), 1)

    def gain_column(j):
        return jnp.sum(jnp.where(lane == j, gcol[...], 0.0), axis=1, keepdims=True)

    @pl.when(first_core)
    def _():
        turn(nat, x_t)
        acc[0:8] = square_sums(0, 32)

    def pass_on(i):
        return pltpu.make_async_remote_copy(
            src_ref=out_t.at[pl.ds(i * 1024, 1024)], dst_ref=x_t.at[pl.ds(i * 1024, 1024)],
            send_sem=cross_send.at[i], recv_sem=cross_recv.at[i], device_id=torus.other(), device_id_type=MESH)

    def pass_back(i):
        return pltpu.make_async_remote_copy(
            src_ref=out_t.at[pl.ds(i * 1024, 1024)], dst_ref=c_t.at[pl.ds(i * 1024, 1024)],
            send_sem=cross_send.at[4 + i], recv_sem=cross_recv.at[4 + i], device_id=torus.other(), device_id_type=MESH)

    @pl.when(second_core)
    def _():
        turn(nat, c_t)
        total = jnp.zeros((8, 256), jnp.float32)
        for i in range(4):
            pass_on(i).wait_recv()
            total = total + square_sums(8 * i, 8)
        acc[0:8] = total

    mean = jnp.sum(acc[0:8], axis=0, keepdims=True) * (1.0 / 4096.0)
    factor = lax.rsqrt(mean + 1e-05)
    stat[0:1] = factor

    def norm_body(j, carry):
        x = x_t[rows(j, 128), :].astype(jnp.float32)
        h = (x * stat[0:1] * gain_column(j)).astype(jnp.bfloat16)
        h_t[rows(j, 128), :] = h
        h_nat[:, rows(j, 128)] = h.T
        return carry

    lax.fori_loop(0, 32, norm_body, 0)

    for c, (_, start, w) in enumerate(COLOURS):
        def project_body(z, total, c=c, w=w):
            weight = jnp.concatenate([chunk_of(bufs, c, z, y)[...].reshape(256, w) for y in range(4)], axis=0)
            return total + dot(h_nat[:, rows(z, 1024)], weight)

        total = lax.fori_loop(0, 4, project_body, jnp.zeros((256, w), jnp.float32))
        kv[:, start:start + w] = total.astype(jnp.bfloat16)
    kv_t[...] = kv[...].T

    scale = HEAD_DIM ** -0.5

    def heads(ref, h, b):
        return jnp.concatenate(
            [ref[rows(h * 8 + j, 128), rows(b, 128)] for j in range(8)], axis=1)

    def forward_body(i, carry):
        h, b = i // 2, lax.rem(i, 2)
        q = heads(h_t, h, b)
        scores = dot(kv[rows(b, 128), rows(h, 128)], q) * scale
        bias = bias_ref[b]
        weights = jnp.exp(scores + jnp.concatenate([bias] * 8, axis=1))
        share = 1.0 / jnp.sum(weights, axis=0, keepdims=True)
        p_t[i] = (weights * share).astype(jnp.bfloat16)
        return carry

    lax.fori_loop(0, 8, forward_body, 0)

    @pl.when(first_core)
    def _():
        for h in range(4):
            for b in range(2):
                mixed = dot(kv_t[512 + 128 * h:640 + 128 * h, 128 * b:128 * b + 128], p_t[2 * h + b])
                for j in range(8):
                    at = (pl.ds((8 * h + j) * 128, 128), pl.ds(b * 128, 128))
                    out_t[at] = (x_t[at].astype(jnp.float32) + mixed[:, 128 * j:128 * j + 128]).astype(jnp.bfloat16)
            pass_on(h).start()
        for i in range(4):
            pass_back(i).wait_recv()

    def backward_body(i, carry):
        h, b = i // 2, lax.rem(i, 2)
        c = heads(c_t, h, b)
        p = p_t[i]
        d_p = dot(kv[rows(b, 128), rows(4 + h, 128)], c)
        p_wide = p.astype(jnp.float32)
        inner = jnp.sum(p_wide * d_p, axis=0, keepdims=True)
        d_s = (p_wide * (d_p - inner) * scale).astype(jnp.bfloat16)
        dkv[rows(b, 128), rows(4 + h, 128)] = dot_nt(p, c).astype(jnp.bfloat16)
        dkv[rows(b, 128), rows(h, 128)] = dot_nt(d_s, heads(h_t, h, b)).astype(jnp.bfloat16)
        d_q = dot(kv_t[rows(h, 128), rows(b, 128)], d_s)
        for j in range(8):
            dh_t[rows(h * 8 + j, 128), rows(b, 128)] = d_q[:, 128 * j:128 * j + 128].astype(jnp.bfloat16)
        return carry

    lax.fori_loop(0, 8, backward_body, 0)
    dkv_t[...] = dkv[...].T

    for c, (_, start, w) in enumerate(COLOURS):
        def grad_body(i, carry, c=c, start=start, w=w):
            z, y = i // 4, lax.rem(i, 4)
            part = dot(h_t[rows(i, 256), :], dkv[:, start:start + w]).astype(jnp.bfloat16)
            chunk_of(sums, c, z, y)[...] = part.reshape(4, ROWS, w)
            return carry

        lax.fori_loop(0, 16, grad_body, 0)

    ggcol[...] = jnp.zeros_like(ggcol)

    def through_body(i, carry):
        z, y = i // 4, lax.rem(i, 4)
        weight = jnp.concatenate(
            [chunk_of(bufs, c, z, y)[...].reshape(256, w) for c, (_, _, w) in enumerate(COLOURS)], axis=1)
        d_h = (dh_t[rows(i, 256), :].astype(jnp.float32) + dot(weight, dkv_t[...])).astype(jnp.bfloat16)
        dh_t[rows(i, 256), :] = d_h
        a = x_t[rows(i, 256), :].astype(jnp.float32)
        both = d_h.astype(jnp.float32) * a
        gains = jnp.concatenate([gain_column(2 * i), gain_column(2 * i + 1)], axis=0)
        by_gain = jnp.sum(both * stat[0:1], axis=1, keepdims=True)
        ggcol[...] = jnp.where(
            lane == 2 * i, by_gain[0:128], jnp.where(lane == 2 * i + 1, by_gain[128:256], ggcol[...]))
        return carry + jnp.sum((both * gains).reshape(32, 8, 256), axis=0)

    dots = lax.fori_loop(0, 16, through_body, jnp.zeros((8, 256), jnp.float32))
    factor = stat[0:1]
    stat[1:2] = factor * factor * factor * jnp.sum(dots, axis=0, keepdims=True) * (1.0 / 4096.0)

    @pl.when(first_core)
    def _():
        for i in range(4):
            pass_on(i).wait_send()

    def flow_body(j, carry):
        u = dh_t[rows(j, 128), :].astype(jnp.float32) * gain_column(j)
        x = x_t[rows(j, 128), :].astype(jnp.float32)
        d_norm = (u * stat[0:1] - x * stat[1:2]).astype(jnp.bfloat16)
        flow = (c_t[rows(j, 128), :].astype(jnp.float32) + d_norm.astype(jnp.float32)).astype(jnp.bfloat16)
        out_t[rows(j, 128), :] = flow
        return carry

    for i in range(4):
        lax.fori_loop(8 * i, 8 * i + 8, flow_body, 0)
        pl.when(second_core)(pass_back(i).start)

    def out_body(i, carry):
        nat[:, rows(i, 512)] = out_t[rows(i, 512), :].T
        return carry

    lax.fori_loop(0, 8, out_body, 0)
    store = pltpu.make_async_copy(nat, out_ref, local_sem.at[7])
    store.start()

    gcol[...] = ggcol[...].T
    for j in range(32):
        i = 2 * j
        row = jnp.broadcast_to(gcol[j:j + 1, :], (8, 128))
        bg[i // 16, i // 4 % 4, i % 4] = row
        bg[i // 16, i // 4 % 4, i % 4 + 1] = row
    inboxes = {2: (r20, r21, r22), 1: (r10, r11, r12), 0: (r00, r01, r02)}
    quick = {2: q2, 1: q1, 0: q0}
    for phase in (2, 1, 0):
        sends += gain_scatter_phase(torus, bg, quick[phase], (sgsend_sem, sgrecv_sem), phase)
        sends += scatter_phase(torus, sums, inboxes[phase], (ssend_sem, srecv_sem), phase)

    def mine(c):
        axes = COLOURS[c][0]
        return block(sums[c], torus, axes, 0, torus.pos[axes[0]])[...].astype(jnp.float32)

    m1 = mine(1)
    key_out[:, 0:384] = mine(0)
    key_out[:, 384:512] = m1[:, 0:128]
    value_out[:, 0:256] = m1[:, 128:384]
    value_out[:, 256:512] = mine(2)
    gain_out[...] = bg[torus.pos["z"], torus.pos["y"], torus.pos["x"]]

    for copy in sends:
        copy.wait_send()
    store.wait()

    @pl.when(second_core)
    def _():
        for i in range(4):
            pass_back(i).wait_send()


def layers(bias, gain_slab, key_weight, value_weight, inputs, upstream):
    vmem = pl.BlockSpec(memory_space=pltpu.VMEM)
    anywhere = pl.BlockSpec(memory_space=pl.ANY)
    bf16, f32 = jnp.bfloat16, jnp.float32
    dma = pltpu.SemaphoreType.DMA
    slabs = [pltpu.VMEM((4, 4, 4, ROWS, w), bf16) for _, _, w in COLOURS] + [pltpu.VMEM((4, 4, 4, 8, 128), f32)]
    return pl.pallas_call(
        layer_kernel,
        out_shape=[
            jax.ShapeDtypeStruct((256, 4096), bf16),
            jax.ShapeDtypeStruct((ROWS, 512), f32),
            jax.ShapeDtypeStruct((ROWS, 512), f32),
            jax.ShapeDtypeStruct((8, 128), f32),
        ],
        in_specs=[vmem, vmem, anywhere, anywhere, anywhere, anywhere],
        out_specs=[anywhere, vmem, vmem, vmem],
        scratch_shapes=slabs + slabs
        + [pltpu.VMEM((6, 2, 4, ROWS, w), bf16) for _, _, w in COLOURS]
        + [pltpu.VMEM((6, 2, ROWS, w), bf16) for _, _, w in COLOURS]
        + [pltpu.VMEM((6, ROWS // 2, w), bf16) for _, _, w in COLOURS]
        + [pltpu.VMEM((3, 4, 4, 8, 128), f32), pltpu.VMEM((3, 4, 8, 128), f32), pltpu.VMEM((3, 8, 128), f32)]
        + [
            pltpu.VMEM((256, 4096), bf16),
            pltpu.VMEM((4096, 256), bf16),
            pltpu.VMEM((4096, 256), bf16),
            pltpu.VMEM((4096, 256), bf16),
            pltpu.VMEM((256, 4096), bf16),
            pltpu.VMEM((4096, 256), bf16),
            pltpu.VMEM((4096, 256), bf16),
            pltpu.VMEM((8, 128, 1024), bf16),
            pltpu.VMEM((256, 1024), bf16),
            pltpu.VMEM((1024, 256), bf16),
            pltpu.VMEM((256, 1024), bf16),
            pltpu.VMEM((1024, 256), bf16),
            pltpu.VMEM((128, 128), f32),
            pltpu.VMEM((128, 128), f32),
            pltpu.VMEM((8, 256), f32),
            pltpu.VMEM((8, 256), f32),
        ]
        + [
            dma((8,)),
            dma((3, 3, 6)), dma((3, 3, 6)), dma((3, 3)), dma((3, 3)),
            dma((3, 3, 6)), dma((3, 3, 6)), dma((3, 3)), dma((3, 3)),
            dma((8,)), dma((8,)),
        ],
        compiler_params=pltpu.CompilerParams(
            collective_id=0, has_side_effects=True, vmem_limit_bytes=58 * 1024 * 1024),
        name="layers",
    )(bias, gain_slab, key_weight, value_weight, inputs, upstream)


def shards(inputs, upstream, doc_blocks, gain, key_weight, value_weight):
    odd = lax.rem(lax.axis_index("dp"), 2) == 1
    row = gain[0].astype(jnp.float32)
    still = jnp.zeros_like(row)
    lanes = jnp.where(odd, jnp.concatenate([still, row]), jnp.concatenate([row, still]))
    slab = jnp.broadcast_to(lanes[None], (8, 128))
    docs = jnp.repeat(doc_blocks, BLOCK, axis=1)
    allowed = (docs[:, :, None] == docs[:, None, :]) & (jnp.arange(128)[:, None] <= jnp.arange(128)[None, :])
    bias = jnp.where(allowed, 0.0, -1e30).astype(jnp.float32)
    flow, key_share, value_share, gain_share = layers(
        bias, slab, key_weight[0], value_weight[0], inputs.reshape(256, 4096), upstream.reshape(256, 4096))
    gain_share = jnp.where(odd, gain_share[0, 64:], gain_share[0, :64])
    return (flow.reshape(1, 2, 128, 4096), key_share[None], value_share[None], gain_share[None])


def solution(mesh):
    in_specs = (
        P("dp", None, None),
        P("dp", None, None),
        P("dp", None),
        P("section", "dp"),
        P("section", "dp", None),
        P("section", "dp", None),
    )
    out_specs = (
        P("section", "dp", None, None),
        P("section", "dp", None),
        P("section", "dp", None),
        P("section", "dp"),
    )
    return jax.shard_map(shards, mesh=mesh, in_specs=in_specs, out_specs=out_specs, check_vma=False)
```

```python
import jax
import jax.numpy as jnp
from jax import lax
from jax.experimental import pallas as pl
from jax.experimental.pallas import tpu as pltpu
from jax.sharding import PartitionSpec as P

HEAD_DIM = 128
BLOCK = 64
ROWS = 64
STRIDE = {"x": 1, "y": 4, "z": 16}
COLOURS = ((("x", "y", "z"), 0, 384), (("z", "y", "x"), 384, 384), (("x", "z", "y"), 768, 256))
OWN, AFTER, FAR, BEFORE = 0, 1, 2, 3
MESH = pl.DeviceIdType.MESH


class Torus:
    def __init__(self):
        self.section = lax.axis_index("section")
        self.me = lax.axis_index("dp")
        self.pos = {"x": lax.rem(self.me, 4), "y": lax.rem(self.me // 4, 4), "z": self.me // 16}

    def at(self, axis, delta):
        return lax.rem(self.pos[axis] + delta, 4)

    def peer(self, axis, delta):
        return (self.section, self.me + (self.at(axis, delta) - self.pos[axis]) * STRIDE[axis])

    def other(self):
        return (1 - self.section, self.me)

    def barrier(self):
        sem = pltpu.get_barrier_semaphore()
        for axis in "xyz":
            for delta in (1, 2, 3):
                pl.semaphore_signal(sem, inc=1, device_id=self.peer(axis, delta), device_id_type=MESH)
        pl.semaphore_signal(sem, inc=1, device_id=self.other(), device_id_type=MESH)
        pl.semaphore_wait(sem, 10)


def remote(src, dst, sems, index, device):
    return pltpu.make_async_remote_copy(
        src_ref=src, dst_ref=dst, send_sem=sems[0].at[index], recv_sem=sems[1].at[index],
        device_id=device, device_id_type=MESH)


def half(ref, which):
    size = ref.shape[0] // 2
    return ref.at[pl.ds(which * size, size)]


def add_into(dst, *others):
    for i in range(dst.shape[0]) if len(dst.shape) > 2 else (Ellipsis,):
        total = dst[i].astype(jnp.float32)
        for other in others:
            total = total + other[i].astype(jnp.float32)
        dst[i] = total.astype(dst.dtype)


class Ring:
    def __init__(self, torus, axis, sems, index, sends):
        self.torus, self.axis, self.sems, self.index, self.sends = torus, axis, sems, index, sends

    def send(self, k, src, dst, delta):
        copy = remote(src, dst, self.sems, self.index + (k,), self.torus.peer(self.axis, delta))
        copy.start()
        self.sends.append(copy)

    def arrived(self, k, ref):
        remote(ref, ref, self.sems, self.index + (k,), self.torus.peer(self.axis, 1)).wait_recv()


class Gather(Ring):
    def __init__(self, torus, axis, sems, index, sends, ref_at):
        super().__init__(torus, axis, sems, index, sends)
        self.blocks = [ref_at(torus.at(axis, d)) for d in range(4)]

    def start(self):
        own = self.blocks[OWN]
        for k, which, delta in ((0, 0, 1), (2, 1, 3), (1, 1, 1), (3, 0, 3)):
            self.send(k, half(own, which), half(own, which), delta)

    def forward(self):
        for k, block, which, delta in ((0, BEFORE, 0, 1), (2, AFTER, 1, 3)):
            ref = half(self.blocks[block], which)
            self.arrived(k, ref)
            self.send(4 + k // 2, ref, ref, delta)

    def near(self):
        self.arrived(1, half(self.blocks[BEFORE], 1))
        self.arrived(3, half(self.blocks[AFTER], 0))

    def finish(self):
        self.arrived(4, half(self.blocks[FAR], 0))
        self.arrived(5, half(self.blocks[FAR], 1))


class Scatter(Ring):
    def __init__(self, torus, axis, sems, index, sends, ref_at, inbox):
        super().__init__(torus, axis, sems, index, sends)
        self.blocks = [ref_at(torus.at(axis, d)) for d in range(4)]
        self.inbox = inbox

    def out(self, k, block, which, delta):
        self.send(k, half(self.blocks[block], which), self.inbox.at[k], delta)

    def into(self, block, which, *slots):
        for k in slots:
            self.arrived(k, self.inbox.at[k])
        add_into(half(self.blocks[block], which), *[self.inbox.at[k] for k in slots])

    def start_far(self):
        self.out(0, FAR, 0, 1)
        self.out(1, FAR, 1, 3)

    def start_after(self):
        self.out(2, AFTER, 1, 1)

    def start_before(self):
        self.out(3, BEFORE, 0, 3)

    def start(self):
        self.start_far()
        self.start_after()
        self.start_before()

    def forward(self):
        self.into(AFTER, 0, 0)
        self.out(4, AFTER, 0, 1)
        self.into(BEFORE, 1, 1)
        self.out(5, BEFORE, 1, 3)

    def finish(self):
        self.into(OWN, 0, 3, 4)
        self.into(OWN, 1, 2, 5)


class Direct:
    def __init__(self, torus, axis, sems, index, sends, ref_at, inbox=None):
        self.ring = Ring(torus, axis, sems, index, sends)
        self.blocks = [ref_at(torus.at(axis, d)) for d in range(4)]
        self.inbox = inbox

    def start(self):
        for k, delta in ((0, 2), (1, 1), (2, 3)):
            if self.inbox is None:
                self.ring.send(k, self.blocks[OWN], self.blocks[OWN], delta)
            else:
                self.ring.send(k, self.blocks[delta], self.inbox.at[k], delta)

    def finish(self):
        for k, delta in ((0, 2), (1, 1), (2, 3)):
            self.ring.arrived(k, self.blocks[4 - delta] if self.inbox is None else self.inbox.at[k])
        if self.inbox is not None:
            add_into(self.blocks[OWN], *[self.inbox.at[k] for k in range(3)])


def chunk_of(bufs, c, z, y):
    index = {"z": z, "y": y, "x": slice(None)}
    first, mid, last = COLOURS[c][0]
    return bufs[c].at[index[last], index[mid], index[first]]


def dot(a, b):
    return jnp.dot(a, b, preferred_element_type=jnp.float32)


def dot_nt(a, b):
    return lax.dot_general(a, b, (((1,), (1,)), ((), ())), preferred_element_type=jnp.float32)


def rows(i, size):
    return pl.ds(pl.multiple_of(i * size, size), size)


def layer_kernel(
    docs_ref, gain_ref, key_ref, value_ref, inputs_ref, upstream_ref,
    out_ref, key_out, value_out, gain_out,
    g0, g1, g2, gg, b0, b1, b2, bg, r20, r21, r22, r10, r11, r12, r00, r01, r02, q2, q1, q0,
    nat, x_t, out_t, m_t, m_nat, c_t, dh_t, p_t, kv, kv_t, dkv, dkv_r, dkv_t, gcol, ggcol, bias, stat,
    local_sem, send_sem, recv_sem, gsend_sem, grecv_sem, ssend_sem, srecv_sem, sgsend_sem, sgrecv_sem, cross_send, cross_recv,
    go_sem,
):
    torus = Torus()
    section, pos = torus.section, torus.pos
    bufs, sums = (g0, g1, g2), (b0, b1, b2)
    first_core, second_core = section == 0, section == 1
    odd = lax.rem(torus.me, 2) == 1
    colours = range(3)
    axes_of = [axes for axes, _, _ in COLOURS]

    def own_place(bufs, c):
        first, mid, last = axes_of[c]
        return bufs[c].at[pos[last], pos[mid], pos[first]]

    local = [
        pltpu.make_async_copy(key_ref.at[:, pl.ds(0, 384)], own_place(bufs, 0), local_sem.at[0]),
        pltpu.make_async_copy(key_ref.at[:, pl.ds(384, 128)], own_place(bufs, 1).at[:, pl.ds(0, 128)], local_sem.at[1]),
        pltpu.make_async_copy(value_ref.at[:, pl.ds(0, 256)], own_place(bufs, 1).at[:, pl.ds(128, 256)], local_sem.at[2]),
        pltpu.make_async_copy(value_ref.at[:, pl.ds(256, 256)], own_place(bufs, 2), local_sem.at[3]),
    ]
    for copy in local:
        copy.start()
    load_inputs = pltpu.make_async_copy(inputs_ref, nat, local_sem.at[5])
    load_upstream = pltpu.make_async_copy(upstream_ref, nat, local_sem.at[6])
    pl.when(first_core)(load_inputs.start)
    pl.when(second_core)(load_upstream.start)
    gain_row = gain_ref[...].astype(jnp.float32)
    still = jnp.zeros_like(gain_row)
    placed = jnp.where(odd, jnp.concatenate([still, gain_row], axis=1), jnp.concatenate([gain_row, still], axis=1))
    gg[pos["z"], pos["y"], pos["x"]] = jnp.broadcast_to(placed, (8, 128))
    torus.barrier()
    for copy in local:
        copy.wait()


    def turn(src, dst, start, count):
        def body(i, carry):
            dst[rows(start + i, 512), :] = src[:, rows(start + i, 512)].T
            return carry

        lax.fori_loop(0, count, body, 0)

    lane = lax.broadcasted_iota(jnp.int32, (128, 128), 1)

    def gain_columns():
        ggcol[...] = jnp.zeros_like(ggcol)
        for j in range(32):
            i = 2 * j
            ggcol[j:j + 1, :] = (gg[i // 16, i // 4 % 4, i % 4] + gg[i // 16, i // 4 % 4, i % 4 + 1])[0:1]
        gcol[...] = ggcol[...].T

    def gain_column(j):
        return jnp.sum(jnp.where(lane == j, gcol[...], 0.0), axis=1, keepdims=True)

    def prepare(start, count):
        def body(i, total):
            x = x_t[rows(start + i, 128), :].astype(jnp.float32)
            m = (x * gain_column(start + i)).astype(jnp.bfloat16)
            m_t[rows(start + i, 128), :] = m
            m_nat[:, rows(start + i, 128)] = m.T
            return total + jnp.sum((x * x).reshape(16, 8, 256), axis=0)

        return lax.fori_loop(0, count, body, jnp.zeros((8, 256), jnp.float32))

    def factors(total):
        mean = jnp.sum(total, axis=0, keepdims=True) * (1.0 / 4096.0)
        stat[0:8] = jnp.broadcast_to(lax.rsqrt(mean + 1e-05), (8, 256))

    def factor_column():
        return stat[0:8].T[:, 0:1]

    def project():
        for c, (_, start, w) in enumerate(COLOURS):
            def body(z, total, c=c, w=w):
                weight = jnp.concatenate([chunk_of(bufs, c, z, y)[...].reshape(256, w) for y in range(4)], axis=0)
                return total + dot(m_nat[:, rows(z, 1024)], weight)

            total = lax.fori_loop(0, 4, body, jnp.zeros((256, w), jnp.float32))
            kv[:, start:start + w] = (total * factor_column()).astype(jnp.bfloat16)
        kv_t[...] = kv[...].T

    def masks():
        key = lax.broadcasted_iota(jnp.int32, (128, 128), 0)
        query = lax.broadcasted_iota(jnp.int32, (128, 128), 1)
        same_block = (key >= BLOCK) == (query >= BLOCK)
        for b in range(2):
            together = jnp.broadcast_to(docs_ref[b, 0] == docs_ref[b, 1], (128, 128))
            allowed = (key <= query) & (same_block | together)
            bias[b] = jnp.where(allowed, 0.0, -1e30)

    scale = HEAD_DIM ** -0.5

    def heads(ref, h, b):
        return jnp.concatenate([ref[rows(h * 8 + j, 128), rows(b, 128)] for j in range(8)], axis=1)

    def token_row(row, b):
        return jnp.concatenate([stat[row:row + 1, rows(b, 128)]] * 8, axis=1)

    def probabilities(i):
        h, b = i // 2, lax.rem(i, 2)
        scores = dot(kv[rows(b, 128), rows(h, 128)], heads(m_t, h, b))
        weights = jnp.exp(scores * (token_row(0, b) * scale) + jnp.concatenate([bias[b]] * 8, axis=1))
        share = 1.0 / jnp.sum(weights, axis=0, keepdims=True)
        p_t[i] = (weights * share).astype(jnp.bfloat16)

    def attention_forward():
        def body(i, carry):
            probabilities(i)
            return carry

        lax.fori_loop(0, 8, body, 0)

    def mix(i):
        h, b = i // 2, i % 2
        mixed = dot(kv_t[512 + 128 * h:640 + 128 * h, 128 * b:128 * b + 128], p_t[i])
        for j in range(8):
            at = (pl.ds((8 * h + j) * 128, 128), pl.ds(b * 128, 128))
            out_t[at] = (x_t[at].astype(jnp.float32) + mixed[:, 128 * j:128 * j + 128]).astype(jnp.bfloat16)

    def attention_backward():
        def body(i, carry):
            h, b = i // 2, lax.rem(i, 2)
            c = heads(c_t, h, b)
            p = p_t[i]
            d_p = dot(kv[rows(b, 128), rows(4 + h, 128)], c)
            p_wide = p.astype(jnp.float32)
            inner = jnp.sum(p_wide * d_p, axis=0, keepdims=True)
            d_s = p_wide * (d_p - inner) * scale
            dkv[rows(b, 128), rows(4 + h, 128)] = dot_nt(p, c).astype(jnp.bfloat16)
            d_s_r = (d_s * token_row(0, b)).astype(jnp.bfloat16)
            dkv[rows(b, 128), rows(h, 128)] = dot_nt(d_s_r, heads(m_t, h, b)).astype(jnp.bfloat16)
            d_q = dot(kv_t[rows(h, 128), rows(b, 128)], d_s.astype(jnp.bfloat16))
            for j in range(8):
                dh_t[rows(h * 8 + j, 128), rows(b, 128)] = d_q[:, 128 * j:128 * j + 128].astype(jnp.bfloat16)
            return carry

        lax.fori_loop(0, 8, body, 0)
        dkv_t[...] = dkv[...].T
        dkv_r[...] = (dkv[...].astype(jnp.float32) * factor_column()).astype(jnp.bfloat16)

    def weight_grads(c, delta):
        axes, start, w = COLOURS[c]
        mid = torus.at(axes[1], delta)

        def body(n, carry):
            z, y = (n, mid) if axes[1] == "y" else (mid, n)
            part = dot(m_t[rows(z * 4 + y, 256), :], dkv_r[:, start:start + w]).astype(jnp.bfloat16)
            chunk_of(sums, c, z, y)[...] = part.reshape(4, ROWS, w)
            return carry

        lax.fori_loop(0, 4, body, 0)

    def through():
        ggcol[...] = jnp.zeros_like(ggcol)

        def body(i, carry):
            z, y = i // 4, lax.rem(i, 4)
            weight = jnp.concatenate(
                [chunk_of(bufs, c, z, y)[...].reshape(256, w) for c, (_, _, w) in enumerate(COLOURS)], axis=1)
            d_h = (dh_t[rows(i, 256), :].astype(jnp.float32) + dot(weight, dkv_t[...])).astype(jnp.bfloat16)
            dh_t[rows(i, 256), :] = d_h
            a = x_t[rows(i, 256), :].astype(jnp.float32)
            both = d_h.astype(jnp.float32) * a
            gains = jnp.concatenate([gain_column(2 * i), gain_column(2 * i + 1)], axis=0)
            by_gain = jnp.sum(both * stat[0:1], axis=1, keepdims=True)
            ggcol[...] = jnp.where(
                lane == 2 * i, by_gain[0:128], jnp.where(lane == 2 * i + 1, by_gain[128:256], ggcol[...]))
            return carry + jnp.sum((both * gains).reshape(32, 8, 256), axis=0)

        dots = lax.fori_loop(0, 16, body, jnp.zeros((8, 256), jnp.float32))
        factor = stat[0:1]
        stat[8:9] = factor * factor * factor * jnp.sum(dots, axis=0, keepdims=True) * (1.0 / 4096.0)

    def flow(start, count):
        def body(i, carry):
            j = start + i
            u = dh_t[rows(j, 128), :].astype(jnp.float32) * gain_column(j)
            x = x_t[rows(j, 128), :].astype(jnp.float32)
            d_norm = (u * stat[0:1] - x * stat[8:9]).astype(jnp.bfloat16)
            total = c_t[rows(j, 128), :].astype(jnp.float32) + d_norm.astype(jnp.float32)
            out_t[rows(j, 128), :] = total.astype(jnp.bfloat16)
            return carry

        lax.fori_loop(0, count, body, 0)

    def turn_back():
        def body(i, carry):
            nat[:, rows(i, 512)] = out_t[rows(i, 512), :].T
            return carry

        lax.fori_loop(0, 8, body, 0)

    def pass_on(i):
        part = pl.ds(i * 1024, 1024)
        return remote(out_t.at[part], x_t.at[part], (cross_send, cross_recv), (i,), torus.other())

    def pass_back(i):
        part = pl.ds(i * 1024, 1024)
        return remote(out_t.at[part], c_t.at[part], (cross_send, cross_recv), (4 + i,), torus.other())

    def gathers(sends):
        sems = (send_sem, recv_sem)

        def phase_one(c):
            first, mid, last = axes_of[c]
            return Direct(torus, first, sems, (c, 0), sends, lambda i: bufs[c].at[pos[last], pos[mid], i])

        def phase_two(c):
            first, mid, last = axes_of[c]
            return Gather(torus, mid, sems, (c, 1), sends, lambda i: bufs[c].at[pos[last], i])

        def phase_three(c, delta):
            first, mid, last = axes_of[c]
            return Gather(
                torus, last, sems, (c, 2 + delta), sends, lambda i: bufs[c].at[i, torus.at(mid, delta)])

        gain_refs = (
            lambda i: gg.at[pos["z"], pos["y"], i], lambda i: gg.at[pos["z"], i], lambda i: gg.at[i])
        gains = [
            Direct(torus, "xyz"[k], (gsend_sem, grecv_sem), (k,), sends, gain_refs[k]) for k in range(3)]
        return ([phase_one(c) for c in colours], [phase_two(c) for c in colours],
                [[phase_three(c, d) for d in range(4)] for c in colours], gains)

    def all_of(items, step):
        for item in items:
            getattr(item, step)()

    @pl.when(first_core)
    def _():
        sends = []
        one, two, three, gains = gathers(sends)
        all_of(one, "start")
        gains[0].start()
        load_inputs.wait()
        turn(nat, x_t, 0, 2)
        for c in colours:
            one[c].finish()
            two[c].start()
            three[c][OWN].start()
        gains[0].finish()
        gains[1].start()
        turn(nat, x_t, 2, 4)
        for c in colours:
            two[c].forward()
            two[c].near()
            three[c][BEFORE].start()
            three[c][AFTER].start()
        gains[1].finish()
        gains[2].start()
        turn(nat, x_t, 6, 2)
        for c in colours:
            three[c][OWN].forward()
            two[c].finish()
            three[c][FAR].start()
        gains[2].finish()
        gain_columns()
        total = prepare(0, 16)
        for c in colours:
            three[c][BEFORE].forward()
            three[c][AFTER].forward()
        total = total + prepare(16, 16)
        for c in colours:
            three[c][FAR].forward()
        pl.semaphore_signal(go_sem, inc=1, device_id=torus.other(), device_id_type=MESH)
        factors(total)
        masks()
        for c in colours:
            all_of(three[c], "near")
            all_of(three[c], "finish")
        for copy in sends:
            copy.wait_send()

    @pl.when(second_core)
    def _():
        sends = []
        one, two, three, gains = gathers(sends)
        all_of(one, "start")
        gains[0].start()
        load_upstream.wait()
        all_of(one, "finish")
        all_of(two, "start")
        gains[0].finish()
        gains[1].start()
        turn(nat, c_t, 0, 4)
        all_of(two, "forward")
        gains[1].finish()
        gains[2].start()
        turn(nat, c_t, 4, 4)
        all_of(two, "near")
        all_of(two, "finish")
        gains[2].finish()
        gain_columns()
        masks()
        pl.semaphore_wait(go_sem, 1)
        for d in range(4):
            for c in colours:
                three[c][d].start()
        for d in range(4):
            for c in colours:
                three[c][d].forward()
        total = jnp.zeros((8, 256), jnp.float32)
        for i in range(4):
            pass_on(i).wait_recv()
            total = total + prepare(8 * i, 8)
        factors(total)
        for c in colours:
            all_of(three[c], "near")
            all_of(three[c], "finish")
        for copy in sends:
            copy.wait_send()

    project()
    attention_forward()

    @pl.when(first_core)
    def _():
        for h in range(4):
            mix(2 * h)
            mix(2 * h + 1)
            pass_on(h).start()
        for i in range(4):
            pass_back(i).wait_recv()

    attention_backward()

    @pl.when(second_core)
    def _():
        through()
        for i in range(4):
            flow(8 * i, 8)
            pass_back(i).start()

    sends = []
    inboxes = ((r00, r01, r02), (r10, r11, r12), (r20, r21, r22))
    sems = (ssend_sem, srecv_sem)

    def last_phase(c, delta):
        first, mid, last = axes_of[c]
        return Scatter(
            torus, last, sems, (c, 2 + delta), sends, lambda i: sums[c].at[i, torus.at(mid, delta)],
            inboxes[2][c].at[delta])

    def mid_phase(c):
        first, mid, last = axes_of[c]
        return Scatter(torus, mid, sems, (c, 1), sends, lambda i: sums[c].at[pos[last], i], inboxes[1][c])

    def first_phase(c):
        first, mid, last = axes_of[c]
        return Direct(
            torus, first, sems, (c, 0), sends, lambda i: sums[c].at[pos[last], pos[mid], i], inboxes[0][c])

    gain_refs = (lambda i: bg.at[pos["z"], pos["y"], i], lambda i: bg.at[pos["z"], i], lambda i: bg.at[i])
    gain_trips = [
        Direct(torus, "xyz"[k], (sgsend_sem, sgrecv_sem), (k,), sends, gain_refs[k], (q0, q1, q2)[k]) for k in range(3)]
    three = [[last_phase(c, d) for d in range(4)] for c in colours]
    two = [mid_phase(c) for c in colours]
    one = [first_phase(c) for c in colours]
    order = (FAR, BEFORE, AFTER, OWN)
    for d in order:
        for c in colours:
            weight_grads(c, d)
            three[c][d].start()

    @pl.when(first_core)
    def _():
        through()
        for i in range(4):
            pass_on(i).wait_send()
        flow(0, 32)

    gcol[...] = ggcol[...].T
    for j in range(32):
        i = 2 * j
        row = jnp.broadcast_to(gcol[j:j + 1, :], (8, 128))
        bg[i // 16, i // 4 % 4, i % 4] = row
        bg[i // 16, i // 4 % 4, i % 4 + 1] = row
    gain_trips[2].start()
    for d in (FAR, BEFORE, AFTER):
        for c in colours:
            three[c][d].forward()
    turn_back()
    store = pltpu.make_async_copy(nat, out_ref, local_sem.at[7])
    store.start()
    gain_trips[2].finish()
    gain_trips[1].start()
    for c in colours:
        three[c][FAR].finish()
        two[c].start_far()
    for c in colours:
        three[c][OWN].forward()
    for c in colours:
        three[c][BEFORE].finish()
        two[c].start_before()
        three[c][AFTER].finish()
        two[c].start_after()
    gain_trips[1].finish()
    gain_trips[0].start()
    for c in colours:
        two[c].forward()
        three[c][OWN].finish()
    for c in colours:
        two[c].finish()
        one[c].start()
    gain_trips[0].finish()
    all_of(one, "finish")

    def mine(c):
        return own_place(sums, c)[...].astype(jnp.float32)

    m1 = mine(1)
    key_out[:, 0:384] = mine(0)
    key_out[:, 384:512] = m1[:, 0:128]
    value_out[:, 0:256] = m1[:, 128:384]
    value_out[:, 256:512] = mine(2)
    slab = bg[pos["z"], pos["y"], pos["x"]][0:1]
    gain_out[...] = jnp.where(odd, slab[:, 64:128], slab[:, 0:64])

    for copy in sends:
        copy.wait_send()
    store.wait()

    @pl.when(second_core)
    def _():
        for i in range(4):
            pass_back(i).wait_send()


def layers(docs, gain, key_weight, value_weight, inputs, upstream):
    vmem = pl.BlockSpec(memory_space=pltpu.VMEM)
    anywhere = pl.BlockSpec(memory_space=pl.ANY)
    bf16, f32 = jnp.bfloat16, jnp.float32
    dma = pltpu.SemaphoreType.DMA
    slabs = [pltpu.VMEM((4, 4, 4, ROWS, w), bf16) for _, _, w in COLOURS] + [pltpu.VMEM((4, 4, 4, 8, 128), f32)]
    return pl.pallas_call(
        layer_kernel,
        out_shape=[
            jax.ShapeDtypeStruct((256, 4096), bf16),
            jax.ShapeDtypeStruct((ROWS, 512), f32),
            jax.ShapeDtypeStruct((ROWS, 512), f32),
            jax.ShapeDtypeStruct((1, ROWS), f32),
        ],
        in_specs=[pl.BlockSpec(memory_space=pltpu.SMEM), vmem, anywhere, anywhere, anywhere, anywhere],
        out_specs=[anywhere, vmem, vmem, vmem],
        scratch_shapes=slabs + slabs
        + [pltpu.VMEM((4, 6, 2, ROWS, w), bf16) for _, _, w in COLOURS]
        + [pltpu.VMEM((6, 2, ROWS, w), bf16) for _, _, w in COLOURS]
        + [pltpu.VMEM((3, ROWS, w), bf16) for _, _, w in COLOURS]
        + [pltpu.VMEM((3, 4, 4, 8, 128), f32), pltpu.VMEM((3, 4, 8, 128), f32), pltpu.VMEM((3, 8, 128), f32)]
        + [
            pltpu.VMEM((256, 4096), bf16),
            pltpu.VMEM((4096, 256), bf16),
            pltpu.VMEM((4096, 256), bf16),
            pltpu.VMEM((4096, 256), bf16),
            pltpu.VMEM((256, 4096), bf16),
            pltpu.VMEM((4096, 256), bf16),
            pltpu.VMEM((4096, 256), bf16),
            pltpu.VMEM((8, 128, 1024), bf16),
            pltpu.VMEM((256, 1024), bf16),
            pltpu.VMEM((1024, 256), bf16),
            pltpu.VMEM((256, 1024), bf16),
            pltpu.VMEM((256, 1024), bf16),
            pltpu.VMEM((1024, 256), bf16),
            pltpu.VMEM((128, 128), f32),
            pltpu.VMEM((128, 128), f32),
            pltpu.VMEM((2, 128, 128), f32),
            pltpu.VMEM((16, 256), f32),
        ]
        + [
            dma((8,)),
            dma((3, 6, 6)), dma((3, 6, 6)), dma((3, 3)), dma((3, 3)),
            dma((3, 6, 6)), dma((3, 6, 6)), dma((3, 3)), dma((3, 3)),
            dma((8,)), dma((8,)),
            pltpu.SemaphoreType.REGULAR,
        ],
        compiler_params=pltpu.CompilerParams(
            collective_id=0, has_side_effects=True, vmem_limit_bytes=58 * 1024 * 1024),
        name="layers",
    )(docs, gain, key_weight, value_weight, inputs, upstream)


def shards(inputs, upstream, doc_blocks, gain, key_weight, value_weight):
    flow, key_share, value_share, gain_share = layers(
        doc_blocks, gain, key_weight[0], value_weight[0], inputs.reshape(256, 4096), upstream.reshape(256, 4096))
    return (flow.reshape(1, 2, 128, 4096), key_share[None], value_share[None], gain_share)


def solution(mesh):
    in_specs = (
        P("dp", None, None),
        P("dp", None, None),
        P("dp", None),
        P("section", "dp"),
        P("section", "dp", None),
        P("section", "dp", None),
    )
    out_specs = (
        P("section", "dp", None, None),
        P("section", "dp", None),
        P("section", "dp", None),
        P("section", "dp"),
    )
    return jax.shard_map(shards, mesh=mesh, in_specs=in_specs, out_specs=out_specs, check_vma=False)
```

```python
import jax
import jax.numpy as jnp
from jax import lax
from jax.experimental import pallas as pl
from jax.experimental.pallas import tpu as pltpu
from jax.sharding import PartitionSpec as P

HEAD_DIM = 128
BLOCK = 64
ROWS = 64
STRIDE = {"x": 1, "y": 4, "z": 16}
COLOURS = ((("x", "y", "z"), 0, 384), (("z", "y", "x"), 384, 384), (("x", "z", "y"), 768, 256))
OWN, AFTER, FAR, BEFORE = 0, 1, 2, 3
MESH = pl.DeviceIdType.MESH


class Torus:
    def __init__(self):
        self.section = lax.axis_index("section")
        self.me = lax.axis_index("dp")
        self.pos = {"x": lax.rem(self.me, 4), "y": lax.rem(self.me // 4, 4), "z": self.me // 16}

    def at(self, axis, delta):
        return lax.rem(self.pos[axis] + delta, 4)

    def peer(self, axis, delta):
        return (self.section, self.me + (self.at(axis, delta) - self.pos[axis]) * STRIDE[axis])

    def other(self):
        return (1 - self.section, self.me)

    def barrier(self):
        sem = pltpu.get_barrier_semaphore()
        for axis in "xyz":
            for delta in (1, 2, 3):
                pl.semaphore_signal(sem, inc=1, device_id=self.peer(axis, delta), device_id_type=MESH)
        pl.semaphore_signal(sem, inc=1, device_id=self.other(), device_id_type=MESH)
        pl.semaphore_wait(sem, 10)


def remote(src, dst, sems, index, device):
    return pltpu.make_async_remote_copy(
        src_ref=src, dst_ref=dst, send_sem=sems[0].at[index], recv_sem=sems[1].at[index],
        device_id=device, device_id_type=MESH)


def half(ref, which):
    size = ref.shape[0] // 2
    return ref.at[pl.ds(which * size, size)]


def add_into(dst, *others):
    for i in range(dst.shape[0]) if len(dst.shape) > 2 else (Ellipsis,):
        total = dst[i].astype(jnp.float32)
        for other in others:
            total = total + other[i].astype(jnp.float32)
        dst[i] = total.astype(dst.dtype)


class Ring:
    def __init__(self, torus, axis, sems, index, sends):
        self.torus, self.axis, self.sems, self.index, self.sends = torus, axis, sems, index, sends

    def send(self, k, src, dst, delta):
        copy = remote(src, dst, self.sems, self.index + (k,), self.torus.peer(self.axis, delta))
        copy.start()
        self.sends.append(copy)

    def arrived(self, k, ref):
        remote(ref, ref, self.sems, self.index + (k,), self.torus.peer(self.axis, 1)).wait_recv()


class Gather(Ring):
    def __init__(self, torus, axis, sems, index, sends, ref_at):
        super().__init__(torus, axis, sems, index, sends)
        self.blocks = [ref_at(torus.at(axis, d)) for d in range(4)]

    def start(self):
        own = self.blocks[OWN]
        for k, which, delta in ((0, 0, 1), (2, 1, 3), (1, 1, 1), (3, 0, 3)):
            self.send(k, half(own, which), half(own, which), delta)

    def forward(self):
        for k, block, which, delta in ((0, BEFORE, 0, 1), (2, AFTER, 1, 3)):
            ref = half(self.blocks[block], which)
            self.arrived(k, ref)
            self.send(4 + k // 2, ref, ref, delta)

    def near(self):
        self.arrived(1, half(self.blocks[BEFORE], 1))
        self.arrived(3, half(self.blocks[AFTER], 0))

    def finish(self):
        self.arrived(4, half(self.blocks[FAR], 0))
        self.arrived(5, half(self.blocks[FAR], 1))


class Scatter(Ring):
    def __init__(self, torus, axis, sems, index, sends, ref_at, inbox):
        super().__init__(torus, axis, sems, index, sends)
        self.blocks = [ref_at(torus.at(axis, d)) for d in range(4)]
        self.inbox = inbox

    def out(self, k, block, which, delta):
        self.send(k, half(self.blocks[block], which), self.inbox.at[k], delta)

    def into(self, block, which, *slots):
        for k in slots:
            self.arrived(k, self.inbox.at[k])
        add_into(half(self.blocks[block], which), *[self.inbox.at[k] for k in slots])

    def start_far(self):
        self.out(0, FAR, 0, 1)
        self.out(1, FAR, 1, 3)

    def start_after(self):
        self.out(2, AFTER, 1, 1)

    def start_before(self):
        self.out(3, BEFORE, 0, 3)

    def start(self):
        self.start_far()
        self.start_after()
        self.start_before()

    def forward(self):
        self.into(AFTER, 0, 0)
        self.out(4, AFTER, 0, 1)
        self.into(BEFORE, 1, 1)
        self.out(5, BEFORE, 1, 3)

    def finish(self):
        self.into(OWN, 0, 3, 4)
        self.into(OWN, 1, 2, 5)


class Direct:
    def __init__(self, torus, axis, sems, index, sends, ref_at, inbox=None):
        self.ring = Ring(torus, axis, sems, index, sends)
        self.blocks = [ref_at(torus.at(axis, d)) for d in range(4)]
        self.inbox = inbox

    def start(self):
        for k, delta in ((0, 2), (1, 1), (2, 3)):
            if self.inbox is None:
                self.ring.send(k, self.blocks[OWN], self.blocks[OWN], delta)
            else:
                self.ring.send(k, self.blocks[delta], self.inbox.at[k], delta)

    def finish(self):
        for k, delta in ((0, 2), (1, 1), (2, 3)):
            self.ring.arrived(k, self.blocks[4 - delta] if self.inbox is None else self.inbox.at[k])
        if self.inbox is not None:
            add_into(self.blocks[OWN], *[self.inbox.at[k] for k in range(3)])


def chunk_of(bufs, c, z, y):
    index = {"z": z, "y": y, "x": slice(None)}
    first, mid, last = COLOURS[c][0]
    return bufs[c].at[index[last], index[mid], index[first]]


def dot(a, b):
    return jnp.dot(a, b, preferred_element_type=jnp.float32)


def dot_nt(a, b):
    return lax.dot_general(a, b, (((1,), (1,)), ((), ())), preferred_element_type=jnp.float32)


def rows(i, size):
    return pl.ds(pl.multiple_of(i * size, size), size)


def layer_kernel(
    docs_ref, gain_ref, key_ref, value_ref, inputs_ref, upstream_ref,
    out_ref, key_out, value_out, gain_out,
    g0, g1, g2, gg, b0, b1, b2, bg, r20, r21, r22, r10, r11, r12, r00, r01, r02, q2, q1, q0,
    nat, x_t, out_t, m_t, m_nat, c_t, dh_t, p_t, kv, kv_t, dkv, dkv_r, dkv_t, gcol, bias, stat,
    local_sem, send_sem, recv_sem, gsend_sem, grecv_sem, ssend_sem, srecv_sem, sgsend_sem, sgrecv_sem, cross_send, cross_recv,
    go_sem,
):
    torus = Torus()
    section, pos = torus.section, torus.pos
    bufs, sums = (g0, g1, g2), (b0, b1, b2)
    first_core, second_core = section == 0, section == 1
    odd = lax.rem(torus.me, 2) == 1
    colours = range(3)
    axes_of = [axes for axes, _, _ in COLOURS]

    def own_place(bufs, c):
        first, mid, last = axes_of[c]
        return bufs[c].at[pos[last], pos[mid], pos[first]]

    local = [
        pltpu.make_async_copy(key_ref.at[:, pl.ds(0, 384)], own_place(bufs, 0), local_sem.at[0]),
        pltpu.make_async_copy(key_ref.at[:, pl.ds(384, 128)], own_place(bufs, 1).at[:, pl.ds(0, 128)], local_sem.at[1]),
        pltpu.make_async_copy(value_ref.at[:, pl.ds(0, 256)], own_place(bufs, 1).at[:, pl.ds(128, 256)], local_sem.at[2]),
        pltpu.make_async_copy(value_ref.at[:, pl.ds(256, 256)], own_place(bufs, 2), local_sem.at[3]),
    ]
    for copy in local:
        copy.start()
    load_inputs = pltpu.make_async_copy(inputs_ref, nat, local_sem.at[5])
    load_upstream = pltpu.make_async_copy(upstream_ref, nat, local_sem.at[6])
    pl.when(first_core)(load_inputs.start)
    pl.when(second_core)(load_upstream.start)
    gain_row = gain_ref[...].astype(jnp.float32)
    still = jnp.zeros_like(gain_row)
    placed = jnp.where(odd, jnp.concatenate([still, gain_row], axis=1), jnp.concatenate([gain_row, still], axis=1))
    gg[pos["z"], pos["y"], pos["x"]] = jnp.broadcast_to(placed, (8, 128))
    torus.barrier()
    for copy in local:
        copy.wait()


    def turn(src, dst, start, count):
        for i in range(start, start + count):
            part = slice(512 * i, 512 * i + 512)
            dst[part, :] = src[:, part].T

    def gain_columns():
        for j in range(32):
            i = 2 * j
            row = gg[i // 16, i // 4 % 4, i % 4] + gg[i // 16, i // 4 % 4, i % 4 + 1]
            gcol[128 * j:128 * j + 128, :] = jnp.broadcast_to(row[0:1], (128, 128)).T.astype(jnp.bfloat16)

    def gains_of(part):
        once = gcol[part, :].astype(jnp.float32)
        return jnp.concatenate([once, once], axis=1)

    def prepare(start, count):
        total = jnp.zeros((8, 256), jnp.float32)
        for i in range(start, start + count):
            part = slice(128 * i, 128 * i + 128)
            x = x_t[part, :].astype(jnp.float32)
            m = (x * gains_of(part)).astype(jnp.bfloat16)
            m_t[part, :] = m
            m_nat[:, part] = m.T
            total = total + jnp.sum((x * x).reshape(16, 8, 256), axis=0)
        return total

    def factors(total):
        mean = jnp.sum(total, axis=0, keepdims=True) * (1.0 / 4096.0)
        stat[0:8] = jnp.broadcast_to(lax.rsqrt(mean + 1e-05), (8, 256))

    def factor_column():
        return stat[0:8].T[:, 0:1]

    def project():
        for c, (_, start, w) in enumerate(COLOURS):
            weight = jnp.concatenate(
                [chunk_of(bufs, c, z, y)[...].reshape(256, w) for z in range(4) for y in range(4)], axis=0)
            kv[:, start:start + w] = (dot(m_nat[...], weight) * factor_column()).astype(jnp.bfloat16)
        kv_t[...] = kv[...].T

    def masks():
        key = lax.broadcasted_iota(jnp.int32, (128, 128), 0)
        query = lax.broadcasted_iota(jnp.int32, (128, 128), 1)
        same_block = (key >= BLOCK) == (query >= BLOCK)
        for b in range(2):
            together = jnp.broadcast_to(docs_ref[b, 0] == docs_ref[b, 1], (128, 128))
            allowed = (key <= query) & (same_block | together)
            bias[b] = jnp.where(allowed, 0.0, -1e30)

    scale = HEAD_DIM ** -0.5

    def heads(ref, h, b):
        return jnp.concatenate([ref[rows(h * 8 + j, 128), rows(b, 128)] for j in range(8)], axis=1)

    def token_row(row, b):
        return jnp.concatenate([stat[row:row + 1, rows(b, 128)]] * 8, axis=1)

    def probabilities(i):
        h, b = i // 2, lax.rem(i, 2)
        scores = dot(kv[rows(b, 128), rows(h, 128)], heads(m_t, h, b))
        weights = jnp.exp(scores * (token_row(0, b) * scale) + jnp.concatenate([bias[b]] * 8, axis=1))
        share = 1.0 / jnp.sum(weights, axis=0, keepdims=True)
        p_t[i] = (weights * share).astype(jnp.bfloat16)

    def attention_forward():
        def body(i, carry):
            probabilities(i)
            return carry

        lax.fori_loop(0, 8, body, 0, unroll=8)

    def mix(i):
        h, b = i // 2, i % 2
        mixed = dot(kv_t[512 + 128 * h:640 + 128 * h, 128 * b:128 * b + 128], p_t[i])
        for j in range(8):
            at = (pl.ds((8 * h + j) * 128, 128), pl.ds(b * 128, 128))
            out_t[at] = (x_t[at].astype(jnp.float32) + mixed[:, 128 * j:128 * j + 128]).astype(jnp.bfloat16)

    def attention_backward():
        def body(i, carry):
            h, b = i // 2, lax.rem(i, 2)
            c = heads(c_t, h, b)
            p = p_t[i]
            d_p = dot(kv[rows(b, 128), rows(4 + h, 128)], c)
            p_wide = p.astype(jnp.float32)
            inner = jnp.sum(p_wide * d_p, axis=0, keepdims=True)
            d_s = p_wide * (d_p - inner) * scale
            dkv[rows(b, 128), rows(4 + h, 128)] = dot_nt(p, c).astype(jnp.bfloat16)
            d_s_r = (d_s * token_row(0, b)).astype(jnp.bfloat16)
            dkv[rows(b, 128), rows(h, 128)] = dot_nt(d_s_r, heads(m_t, h, b)).astype(jnp.bfloat16)
            d_q = dot(kv_t[rows(h, 128), rows(b, 128)], d_s.astype(jnp.bfloat16))
            for j in range(8):
                dh_t[rows(h * 8 + j, 128), rows(b, 128)] = d_q[:, 128 * j:128 * j + 128].astype(jnp.bfloat16)
            return carry

        lax.fori_loop(0, 8, body, 0, unroll=8)
        dkv_t[...] = dkv[...].T
        dkv_r[...] = (dkv[...].astype(jnp.float32) * factor_column()).astype(jnp.bfloat16)

    def weight_grads(c, delta):
        axes, start, w = COLOURS[c]
        mid = torus.at(axes[1], delta)

        for n in range(4):
            z, y = (n, mid) if axes[1] == "y" else (mid, n)
            part = dot(m_t[rows(z * 4 + y, 256), :], dkv_r[:, start:start + w]).astype(jnp.bfloat16)
            chunk_of(sums, c, z, y)[...] = part.reshape(4, ROWS, w)

    def through():
        factor = stat[0:1]
        dots = jnp.zeros((8, 256), jnp.float32)
        for i in range(16):
            z, y = i // 4, i % 4
            part = slice(256 * i, 256 * i + 256)
            weight = jnp.concatenate(
                [chunk_of(bufs, c, z, y)[...].reshape(256, w) for c, (_, _, w) in enumerate(COLOURS)], axis=1)
            d_h = (dh_t[part, :].astype(jnp.float32) + dot(weight, dkv_t[...])).astype(jnp.bfloat16)
            dh_t[part, :] = d_h
            both = d_h.astype(jnp.float32) * x_t[part, :].astype(jnp.float32)
            dots = dots + jnp.sum((both * gains_of(part)).reshape(32, 8, 256), axis=0)
        stat[8:9] = factor * factor * factor * jnp.sum(dots, axis=0, keepdims=True) * (1.0 / 4096.0)

    def gain_grads():
        lane = lax.broadcasted_iota(jnp.int32, (128, 128), 1)
        total = jnp.zeros((128, 128), jnp.float32)
        for j in range(32):
            part = slice(128 * j, 128 * j + 128)
            each = dh_t[part, :].astype(jnp.float32) * x_t[part, :].astype(jnp.float32) * stat[0:1]
            total = jnp.where(lane == j, jnp.sum(each, axis=1, keepdims=True), total)
        total = total.T
        for j in range(32):
            i = 2 * j
            row = jnp.broadcast_to(total[j:j + 1, :], (8, 128))
            bg[i // 16, i // 4 % 4, i % 4] = row
            bg[i // 16, i // 4 % 4, i % 4 + 1] = row

    def flow(start, count):
        for i in range(start, start + count):
            part = slice(128 * i, 128 * i + 128)
            u = dh_t[part, :].astype(jnp.float32) * gains_of(part)
            x = x_t[part, :].astype(jnp.float32)
            d_norm = (u * stat[0:1] - x * stat[8:9]).astype(jnp.bfloat16)
            out_t[part, :] = (c_t[part, :].astype(jnp.float32) + d_norm.astype(jnp.float32)).astype(jnp.bfloat16)

    def turn_back():
        for i in range(8):
            part = slice(512 * i, 512 * i + 512)
            nat[:, part] = out_t[part, :].T

    def pass_on(i):
        part = pl.ds(i * 1024, 1024)
        return remote(out_t.at[part], x_t.at[part], (cross_send, cross_recv), (i,), torus.other())

    def pass_back(i):
        part = pl.ds(i * 1024, 1024)
        return remote(out_t.at[part], c_t.at[part], (cross_send, cross_recv), (4 + i,), torus.other())

    def gathers(sends):
        sems = (send_sem, recv_sem)

        def phase_one(c):
            first, mid, last = axes_of[c]
            return Direct(torus, first, sems, (c, 0), sends, lambda i: bufs[c].at[pos[last], pos[mid], i])

        def phase_two(c):
            first, mid, last = axes_of[c]
            return Gather(torus, mid, sems, (c, 1), sends, lambda i: bufs[c].at[pos[last], i])

        def phase_three(c, delta):
            first, mid, last = axes_of[c]
            return Gather(
                torus, last, sems, (c, 2 + delta), sends, lambda i: bufs[c].at[i, torus.at(mid, delta)])

        gain_refs = (
            lambda i: gg.at[pos["z"], pos["y"], i], lambda i: gg.at[pos["z"], i], lambda i: gg.at[i])
        gains = [
            Direct(torus, "xyz"[k], (gsend_sem, grecv_sem), (k,), sends, gain_refs[k]) for k in range(3)]
        return ([phase_one(c) for c in colours], [phase_two(c) for c in colours],
                [[phase_three(c, d) for d in range(4)] for c in colours], gains)

    def all_of(items, step):
        for item in items:
            getattr(item, step)()

    @pl.when(first_core)
    def _():
        sends = []
        one, two, three, gains = gathers(sends)
        all_of(one, "start")
        gains[0].start()
        load_inputs.wait()
        turn(nat, x_t, 0, 2)
        for c in colours:
            one[c].finish()
            two[c].start()
            three[c][OWN].start()
        gains[0].finish()
        gains[1].start()
        turn(nat, x_t, 2, 4)
        for c in colours:
            two[c].forward()
            two[c].near()
            three[c][BEFORE].start()
            three[c][AFTER].start()
        gains[1].finish()
        gains[2].start()
        turn(nat, x_t, 6, 2)
        for c in colours:
            three[c][OWN].forward()
            two[c].finish()
            three[c][FAR].start()
        gains[2].finish()
        gain_columns()
        total = prepare(0, 16)
        for c in colours:
            three[c][BEFORE].forward()
            three[c][AFTER].forward()
        total = total + prepare(16, 16)
        for c in colours:
            three[c][FAR].forward()
        pl.semaphore_signal(go_sem, inc=1, device_id=torus.other(), device_id_type=MESH)
        factors(total)
        masks()
        for c in colours:
            all_of(three[c], "near")
            all_of(three[c], "finish")
        for copy in sends:
            copy.wait_send()

    @pl.when(second_core)
    def _():
        sends = []
        one, two, three, gains = gathers(sends)
        all_of(one, "start")
        gains[0].start()
        load_upstream.wait()
        all_of(one, "finish")
        all_of(two, "start")
        gains[0].finish()
        gains[1].start()
        turn(nat, c_t, 0, 4)
        all_of(two, "forward")
        gains[1].finish()
        gains[2].start()
        turn(nat, c_t, 4, 4)
        all_of(two, "near")
        all_of(two, "finish")
        gains[2].finish()
        gain_columns()
        masks()
        pl.semaphore_wait(go_sem, 1)
        for d in range(4):
            for c in colours:
                three[c][d].start()
        for d in range(4):
            for c in colours:
                three[c][d].forward()
        total = jnp.zeros((8, 256), jnp.float32)
        for i in range(4):
            pass_on(i).wait_recv()
            total = total + prepare(8 * i, 8)
        factors(total)
        for c in colours:
            all_of(three[c], "near")
            all_of(three[c], "finish")
        for copy in sends:
            copy.wait_send()

    project()
    attention_forward()

    @pl.when(first_core)
    def _():
        for h in range(4):
            mix(2 * h)
            mix(2 * h + 1)
            pass_on(h).start()
        for i in range(4):
            pass_back(i).wait_recv()

    attention_backward()

    @pl.when(second_core)
    def _():
        through()
        for i in range(4):
            flow(8 * i, 8)
            pass_back(i).start()

    sends = []
    inboxes = ((r00, r01, r02), (r10, r11, r12), (r20, r21, r22))
    sems = (ssend_sem, srecv_sem)

    def last_phase(c, delta):
        first, mid, last = axes_of[c]
        return Scatter(
            torus, last, sems, (c, 2 + delta), sends, lambda i: sums[c].at[i, torus.at(mid, delta)],
            inboxes[2][c].at[delta])

    def mid_phase(c):
        first, mid, last = axes_of[c]
        return Scatter(torus, mid, sems, (c, 1), sends, lambda i: sums[c].at[pos[last], i], inboxes[1][c])

    def first_phase(c):
        first, mid, last = axes_of[c]
        return Direct(
            torus, first, sems, (c, 0), sends, lambda i: sums[c].at[pos[last], pos[mid], i], inboxes[0][c])

    gain_refs = (lambda i: bg.at[pos["z"], pos["y"], i], lambda i: bg.at[pos["z"], i], lambda i: bg.at[i])
    gain_trips = [
        Direct(torus, "xyz"[k], (sgsend_sem, sgrecv_sem), (k,), sends, gain_refs[k], (q0, q1, q2)[k]) for k in range(3)]
    three = [[last_phase(c, d) for d in range(4)] for c in colours]
    two = [mid_phase(c) for c in colours]
    one = [first_phase(c) for c in colours]
    order = (FAR, BEFORE, AFTER, OWN)
    for d in order:
        for c in colours:
            weight_grads(c, d)
            three[c][d].start()

    @pl.when(first_core)
    def _():
        through()
        for i in range(4):
            pass_on(i).wait_send()
        flow(0, 32)

    gain_grads()
    gain_trips[2].start()
    for d in (FAR, BEFORE, AFTER):
        for c in colours:
            three[c][d].forward()
    turn_back()
    store = pltpu.make_async_copy(nat, out_ref, local_sem.at[7])
    store.start()
    gain_trips[2].finish()
    gain_trips[1].start()
    for c in colours:
        three[c][FAR].finish()
        two[c].start_far()
    for c in colours:
        three[c][OWN].forward()
    for c in colours:
        three[c][BEFORE].finish()
        two[c].start_before()
        three[c][AFTER].finish()
        two[c].start_after()
    gain_trips[1].finish()
    gain_trips[0].start()
    for c in colours:
        two[c].forward()
        three[c][OWN].finish()
    for c in colours:
        two[c].finish()
        one[c].start()
    gain_trips[0].finish()
    all_of(one, "finish")

    def mine(c):
        return own_place(sums, c)[...].astype(jnp.float32)

    m1 = mine(1)
    key_out[:, 0:384] = mine(0)
    key_out[:, 384:512] = m1[:, 0:128]
    value_out[:, 0:256] = m1[:, 128:384]
    value_out[:, 256:512] = mine(2)
    slab = bg[pos["z"], pos["y"], pos["x"]][0:1]
    gain_out[...] = jnp.where(odd, slab[:, 64:128], slab[:, 0:64])

    for copy in sends:
        copy.wait_send()
    store.wait()

    @pl.when(second_core)
    def _():
        for i in range(4):
            pass_back(i).wait_send()


def layers(docs, gain, key_weight, value_weight, inputs, upstream):
    vmem = pl.BlockSpec(memory_space=pltpu.VMEM)
    anywhere = pl.BlockSpec(memory_space=pl.ANY)
    bf16, f32 = jnp.bfloat16, jnp.float32
    dma = pltpu.SemaphoreType.DMA
    slabs = [pltpu.VMEM((4, 4, 4, ROWS, w), bf16) for _, _, w in COLOURS] + [pltpu.VMEM((4, 4, 4, 8, 128), f32)]
    return pl.pallas_call(
        layer_kernel,
        out_shape=[
            jax.ShapeDtypeStruct((256, 4096), bf16),
            jax.ShapeDtypeStruct((ROWS, 512), f32),
            jax.ShapeDtypeStruct((ROWS, 512), f32),
            jax.ShapeDtypeStruct((1, ROWS), f32),
        ],
        in_specs=[pl.BlockSpec(memory_space=pltpu.SMEM), vmem, anywhere, anywhere, anywhere, anywhere],
        out_specs=[anywhere, vmem, vmem, vmem],
        scratch_shapes=slabs + slabs
        + [pltpu.VMEM((4, 6, 2, ROWS, w), bf16) for _, _, w in COLOURS]
        + [pltpu.VMEM((6, 2, ROWS, w), bf16) for _, _, w in COLOURS]
        + [pltpu.VMEM((3, ROWS, w), bf16) for _, _, w in COLOURS]
        + [pltpu.VMEM((3, 4, 4, 8, 128), f32), pltpu.VMEM((3, 4, 8, 128), f32), pltpu.VMEM((3, 8, 128), f32)]
        + [
            pltpu.VMEM((256, 4096), bf16),
            pltpu.VMEM((4096, 256), bf16),
            pltpu.VMEM((4096, 256), bf16),
            pltpu.VMEM((4096, 256), bf16),
            pltpu.VMEM((256, 4096), bf16),
            pltpu.VMEM((4096, 256), bf16),
            pltpu.VMEM((4096, 256), bf16),
            pltpu.VMEM((8, 128, 1024), bf16),
            pltpu.VMEM((256, 1024), bf16),
            pltpu.VMEM((1024, 256), bf16),
            pltpu.VMEM((256, 1024), bf16),
            pltpu.VMEM((256, 1024), bf16),
            pltpu.VMEM((1024, 256), bf16),
            pltpu.VMEM((4096, 128), bf16),
            pltpu.VMEM((2, 128, 128), f32),
            pltpu.VMEM((16, 256), f32),
        ]
        + [
            dma((8,)),
            dma((3, 6, 6)), dma((3, 6, 6)), dma((3, 3)), dma((3, 3)),
            dma((3, 6, 6)), dma((3, 6, 6)), dma((3, 3)), dma((3, 3)),
            dma((8,)), dma((8,)),
            pltpu.SemaphoreType.REGULAR,
        ],
        compiler_params=pltpu.CompilerParams(
            collective_id=0, has_side_effects=True, vmem_limit_bytes=58 * 1024 * 1024),
        name="layers",
    )(docs, gain, key_weight, value_weight, inputs, upstream)


def shards(inputs, upstream, doc_blocks, gain, key_weight, value_weight):
    flow, key_share, value_share, gain_share = layers(
        doc_blocks, gain, key_weight[0], value_weight[0], inputs.reshape(256, 4096), upstream.reshape(256, 4096))
    return (flow.reshape(1, 2, 128, 4096), key_share[None], value_share[None], gain_share)


def solution(mesh):
    in_specs = (
        P("dp", None, None),
        P("dp", None, None),
        P("dp", None),
        P("section", "dp"),
        P("section", "dp", None),
        P("section", "dp", None),
    )
    out_specs = (
        P("section", "dp", None, None),
        P("section", "dp", None),
        P("section", "dp", None),
        P("section", "dp"),
    )
    return jax.shard_map(shards, mesh=mesh, in_specs=in_specs, out_specs=out_specs, check_vma=False)
```

```python
import jax
import jax.numpy as jnp
from jax import lax
from jax.experimental import pallas as pl
from jax.experimental.pallas import tpu as pltpu
from jax.sharding import PartitionSpec as P

HEAD_DIM = 128
BLOCK = 64
ROWS = 64
STRIDE = {"x": 1, "y": 4, "z": 16}
COLOURS = ((("x", "y", "z"), 0, 384), (("z", "y", "x"), 384, 384), (("x", "z", "y"), 768, 256))
OWN, AFTER, FAR, BEFORE = 0, 1, 2, 3
MESH = pl.DeviceIdType.MESH


class Torus:
    def __init__(self):
        self.section = lax.axis_index("section")
        self.me = lax.axis_index("dp")
        self.pos = {"x": lax.rem(self.me, 4), "y": lax.rem(self.me // 4, 4), "z": self.me // 16}

    def at(self, axis, delta):
        return lax.rem(self.pos[axis] + delta, 4)

    def peer(self, axis, delta):
        return (self.section, self.me + (self.at(axis, delta) - self.pos[axis]) * STRIDE[axis])

    def other(self):
        return (1 - self.section, self.me)

    def barrier(self):
        sem = pltpu.get_barrier_semaphore()
        for axis in "xyz":
            for delta in (1, 2, 3):
                pl.semaphore_signal(sem, inc=1, device_id=self.peer(axis, delta), device_id_type=MESH)
        pl.semaphore_signal(sem, inc=1, device_id=self.other(), device_id_type=MESH)
        pl.semaphore_wait(sem, 10)


def remote(src, dst, sems, index, device):
    return pltpu.make_async_remote_copy(
        src_ref=src, dst_ref=dst, send_sem=sems[0].at[index], recv_sem=sems[1].at[index],
        device_id=device, device_id_type=MESH)


def half(ref, which):
    size = ref.shape[0] // 2
    return ref.at[pl.ds(which * size, size)]


def add_into(dst, *others):
    for i in range(dst.shape[0]) if len(dst.shape) > 2 else (Ellipsis,):
        total = dst[i].astype(jnp.float32)
        for other in others:
            total = total + other[i].astype(jnp.float32)
        dst[i] = total.astype(dst.dtype)


class Ring:
    def __init__(self, torus, axis, sems, index, ref_at, inbox=None):
        self.torus, self.axis, self.sems, self.index, self.inbox = torus, axis, sems, index, inbox
        self.blocks = [ref_at(torus.at(axis, d)) for d in range(4)]

    def copy(self, k, src, dst, delta):
        return remote(src, dst, self.sems, self.index + (k,), self.torus.peer(self.axis, delta))

    def arrived(self, k, ref):
        self.copy(k, ref, ref, 1).wait_recv()


class Gather(Ring):
    def send(self, k, block, which, delta):
        ref = half(self.blocks[block], which)
        self.copy(k, ref, ref, delta).start()

    def start(self):
        self.send(0, OWN, 0, 1)
        self.send(2, OWN, 1, 3)
        self.send(1, OWN, 1, 1)
        self.send(3, OWN, 0, 3)

    def forward(self):
        self.arrived(0, half(self.blocks[BEFORE], 0))
        self.send(4, BEFORE, 0, 1)
        self.arrived(2, half(self.blocks[AFTER], 1))
        self.send(5, AFTER, 1, 3)

    def finish(self):
        self.arrived(1, half(self.blocks[BEFORE], 1))
        self.arrived(3, half(self.blocks[AFTER], 0))
        self.arrived(4, half(self.blocks[FAR], 0))
        self.arrived(5, half(self.blocks[FAR], 1))

    def sent(self):
        ref = half(self.blocks[OWN], 0)
        for k in range(6):
            self.copy(k, ref, ref, 1).wait_send()


class Scatter(Ring):
    def send(self, k, block, which, delta):
        self.copy(k, half(self.blocks[block], which), self.inbox.at[k], delta).start()

    def into(self, block, which, *slots):
        for k in slots:
            self.arrived(k, self.inbox.at[k])
        add_into(half(self.blocks[block], which), *[self.inbox.at[k] for k in slots])

    def start(self):
        self.send(0, FAR, 0, 1)
        self.send(1, FAR, 1, 3)
        self.send(2, AFTER, 1, 1)
        self.send(3, BEFORE, 0, 3)

    def forward(self):
        self.into(AFTER, 0, 0)
        self.send(4, AFTER, 0, 1)
        self.into(BEFORE, 1, 1)
        self.send(5, BEFORE, 1, 3)

    def finish(self):
        self.into(OWN, 0, 3, 4)
        self.into(OWN, 1, 2, 5)

    def sent(self):
        for k in range(6):
            self.copy(k, self.inbox.at[k], self.inbox.at[k], 1).wait_send()


class Direct(Ring):
    def send(self, delta):
        if self.inbox is None:
            self.copy(delta, self.blocks[OWN], self.blocks[OWN], delta).start()
        else:
            self.copy(delta, self.blocks[delta], self.inbox.at[delta], delta).start()

    def start(self):
        for delta in (FAR, AFTER, BEFORE):
            self.send(delta)

    def take(self, block):
        self.arrived(4 - block, self.blocks[block])

    def finish(self):
        if self.inbox is None:
            for block in (AFTER, BEFORE, FAR):
                self.take(block)
        else:
            for k in (1, 3, 2):
                self.arrived(k, self.inbox.at[k])
            add_into(self.blocks[OWN], *[self.inbox.at[k] for k in (1, 2, 3)])

    def sent(self):
        for k in (1, 2, 3):
            self.copy(k, self.blocks[OWN], self.blocks[OWN], 1).wait_send()


def chunk_of(bufs, c, z, y):
    index = {"z": z, "y": y, "x": slice(None)}
    first, mid, last = COLOURS[c][0]
    return bufs[c].at[index[last], index[mid], index[first]]


def dot(a, b):
    return jnp.dot(a, b, preferred_element_type=jnp.float32)


def dot_nt(a, b):
    return lax.dot_general(a, b, (((1,), (1,)), ((), ())), preferred_element_type=jnp.float32)


def rows(i, size):
    if isinstance(i, int):
        return pl.ds(i * size, size)
    return pl.ds(pl.multiple_of(i * size, size), size)


def layer_kernel(
    docs_ref, gain_ref, key_ref, value_ref, inputs_ref, upstream_ref,
    out_ref, key_out, value_out, gain_out,
    g0, g1, g2, gg, b0, b1, b2, bg, r20, r21, r22, r10, r11, r12, r00, r01, r02, q2, q1, q0,
    nat, x_t, out_t, m_t, m_nat, c_t, dh_t, p_t, kv, kv_t, dkv, dkv_r, dkv_t, gcol, bias, stat,
    local_sem, send_sem, recv_sem, gsend_sem, grecv_sem, ssend_sem, srecv_sem, sgsend_sem, sgrecv_sem, cross_send, cross_recv,
    go_sem,
):
    torus = Torus()
    section, pos = torus.section, torus.pos
    bufs, sums = (g0, g1, g2), (b0, b1, b2)
    first_core, second_core = section == 0, section == 1
    odd = lax.rem(torus.me, 2) == 1
    colours = range(3)
    axes_of = [axes for axes, _, _ in COLOURS]

    def own_place(bufs, c):
        first, mid, last = axes_of[c]
        return bufs[c].at[pos[last], pos[mid], pos[first]]

    local = [
        pltpu.make_async_copy(key_ref.at[:, pl.ds(0, 384)], own_place(bufs, 0), local_sem.at[0]),
        pltpu.make_async_copy(key_ref.at[:, pl.ds(384, 128)], own_place(bufs, 1).at[:, pl.ds(0, 128)], local_sem.at[1]),
        pltpu.make_async_copy(value_ref.at[:, pl.ds(0, 256)], own_place(bufs, 1).at[:, pl.ds(128, 256)], local_sem.at[2]),
        pltpu.make_async_copy(value_ref.at[:, pl.ds(256, 256)], own_place(bufs, 2), local_sem.at[3]),
    ]
    for copy in local:
        copy.start()
    load_inputs = pltpu.make_async_copy(inputs_ref, nat, local_sem.at[5])
    load_upstream = pltpu.make_async_copy(upstream_ref, nat, local_sem.at[6])
    pl.when(first_core)(load_inputs.start)
    pl.when(second_core)(load_upstream.start)
    gain_row = gain_ref[...].astype(jnp.float32)
    still = jnp.zeros_like(gain_row)
    placed = jnp.where(odd, jnp.concatenate([still, gain_row], axis=1), jnp.concatenate([gain_row, still], axis=1))
    gg[pos["z"], pos["y"], pos["x"]] = jnp.broadcast_to(placed, (8, 128))
    torus.barrier()
    for copy in local:
        copy.wait()


    def turn(src, dst, start, count):
        for i in range(start, start + count):
            part = slice(512 * i, 512 * i + 512)
            dst[part, :] = src[:, part].T

    def gain_columns():
        for j in range(32):
            i = 2 * j
            row = gg[i // 16, i // 4 % 4, i % 4] + gg[i // 16, i // 4 % 4, i % 4 + 1]
            gcol[128 * j:128 * j + 128, :] = jnp.broadcast_to(row[0:1], (128, 128)).T.astype(jnp.bfloat16)

    def gains_of(part):
        once = gcol[part, :].astype(jnp.float32)
        return jnp.concatenate([once, once], axis=1)

    def prepare(start, count):
        total = jnp.zeros((8, 256), jnp.float32)
        for i in range(start, start + count):
            part = slice(128 * i, 128 * i + 128)
            x = x_t[part, :].astype(jnp.float32)
            m = (x * gains_of(part)).astype(jnp.bfloat16)
            m_t[part, :] = m
            m_nat[:, part] = m.T
            total = total + jnp.sum((x * x).reshape(16, 8, 256), axis=0)
        return total

    def factors(total):
        mean = jnp.sum(total, axis=0, keepdims=True) * (1.0 / 4096.0)
        stat[0:8] = jnp.broadcast_to(lax.rsqrt(mean + 1e-05), (8, 256))

    def factor_column():
        return stat[0:8].T[:, 0:1]

    def project(c):
        _, start, w = COLOURS[c]
        weight = jnp.concatenate(
            [chunk_of(bufs, c, z, y)[...].reshape(256, w) for z in range(4) for y in range(4)], axis=0)
        kv[:, start:start + w] = (dot(m_nat[...], weight) * factor_column()).astype(jnp.bfloat16)

    def masks():
        key = lax.broadcasted_iota(jnp.int32, (128, 128), 0)
        query = lax.broadcasted_iota(jnp.int32, (128, 128), 1)
        same_block = (key >= BLOCK) == (query >= BLOCK)
        for b in range(2):
            together = jnp.broadcast_to(docs_ref[b, 0] == docs_ref[b, 1], (128, 128))
            allowed = (key <= query) & (same_block | together)
            bias[b] = jnp.where(allowed, 0.0, -1e30)

    scale = HEAD_DIM ** -0.5

    def heads(ref, h, b):
        return jnp.concatenate([ref[rows(h * 8 + j, 128), rows(b, 128)] for j in range(8)], axis=1)

    def token_row(row, b):
        return jnp.concatenate([stat[row:row + 1, rows(b, 128)]] * 8, axis=1)

    def attention_forward():
        for i in range(8):
            h, b = i // 2, i % 2
            scores = dot(kv[rows(b, 128), rows(h, 128)], heads(m_t, h, b))
            weights = jnp.exp(scores * (token_row(0, b) * scale) + jnp.concatenate([bias[b]] * 8, axis=1))
            share = 1.0 / jnp.sum(weights, axis=0, keepdims=True)
            p_t[i] = (weights * share).astype(jnp.bfloat16)

    def mix(i):
        h, b = i // 2, i % 2
        mixed = dot(kv_t[512 + 128 * h:640 + 128 * h, 128 * b:128 * b + 128], p_t[i])
        for j in range(8):
            at = (pl.ds((8 * h + j) * 128, 128), pl.ds(b * 128, 128))
            out_t[at] = (x_t[at].astype(jnp.float32) + mixed[:, 128 * j:128 * j + 128]).astype(jnp.bfloat16)

    def attention_backward():
        for i in range(8):
            h, b = i // 2, i % 2
            if b == 0:
                pl.when(first_core)(pass_back(h).wait_recv)
            c = heads(c_t, h, b)
            p = p_t[i]
            d_p = dot(kv[rows(b, 128), rows(4 + h, 128)], c)
            p_wide = p.astype(jnp.float32)
            inner = jnp.sum(p_wide * d_p, axis=0, keepdims=True)
            d_s = p_wide * (d_p - inner) * scale
            dkv[rows(b, 128), rows(4 + h, 128)] = dot_nt(p, c).astype(jnp.bfloat16)
            d_s_r = (d_s * token_row(0, b)).astype(jnp.bfloat16)
            dkv[rows(b, 128), rows(h, 128)] = dot_nt(d_s_r, heads(m_t, h, b)).astype(jnp.bfloat16)
            d_q = dot(kv_t[rows(h, 128), rows(b, 128)], d_s.astype(jnp.bfloat16))
            for j in range(8):
                dh_t[rows(h * 8 + j, 128), rows(b, 128)] = d_q[:, 128 * j:128 * j + 128].astype(jnp.bfloat16)
        dkv_t[...] = dkv[...].T
        dkv_r[...] = (dkv[...].astype(jnp.float32) * factor_column()).astype(jnp.bfloat16)

    def weight_grads(c, delta):
        axes, start, w = COLOURS[c]
        mid = torus.at(axes[1], delta)

        for n in range(4):
            z, y = (n, mid) if axes[1] == "y" else (mid, n)
            part = dot(m_t[rows(z * 4 + y, 256), :], dkv_r[:, start:start + w]).astype(jnp.bfloat16)
            chunk_of(sums, c, z, y)[...] = part.reshape(4, ROWS, w)

    def through():
        factor = stat[0:1]
        dots = jnp.zeros((8, 256), jnp.float32)
        for i in range(16):
            z, y = i // 4, i % 4
            part = slice(256 * i, 256 * i + 256)
            weight = jnp.concatenate(
                [chunk_of(bufs, c, z, y)[...].reshape(256, w) for c, (_, _, w) in enumerate(COLOURS)], axis=1)
            d_h = (dh_t[part, :].astype(jnp.float32) + dot(weight, dkv_t[...])).astype(jnp.bfloat16)
            dh_t[part, :] = d_h
            both = d_h.astype(jnp.float32) * x_t[part, :].astype(jnp.float32)
            dots = dots + jnp.sum((both * gains_of(part)).reshape(32, 8, 256), axis=0)
        stat[8:9] = factor * factor * factor * jnp.sum(dots, axis=0, keepdims=True) * (1.0 / 4096.0)

    def gain_grads():
        lane = lax.broadcasted_iota(jnp.int32, (128, 128), 1)
        total = jnp.zeros((128, 128), jnp.float32)
        for j in range(32):
            part = slice(128 * j, 128 * j + 128)
            each = dh_t[part, :].astype(jnp.float32) * x_t[part, :].astype(jnp.float32) * stat[0:1]
            total = jnp.where(lane == j, jnp.sum(each, axis=1, keepdims=True), total)
        total = total.T
        for j in range(32):
            i = 2 * j
            row = jnp.broadcast_to(total[j:j + 1, :], (8, 128))
            bg[i // 16, i // 4 % 4, i % 4] = row
            bg[i // 16, i // 4 % 4, i % 4 + 1] = row

    def flow(start, count):
        for i in range(start, start + count):
            part = slice(128 * i, 128 * i + 128)
            u = dh_t[part, :].astype(jnp.float32) * gains_of(part)
            x = x_t[part, :].astype(jnp.float32)
            d_norm = (u * stat[0:1] - x * stat[8:9]).astype(jnp.bfloat16)
            out_t[part, :] = (c_t[part, :].astype(jnp.float32) + d_norm.astype(jnp.float32)).astype(jnp.bfloat16)

    def turn_back():
        for i in range(8):
            part = slice(512 * i, 512 * i + 512)
            nat[:, part] = out_t[part, :].T

    def pass_on(i):
        part = pl.ds(i * 1024, 1024)
        return remote(out_t.at[part], x_t.at[part], (cross_send, cross_recv), (i,), torus.other())

    def pass_back(i):
        part = pl.ds(i * 1024, 1024)
        return remote(out_t.at[part], c_t.at[part], (cross_send, cross_recv), (4 + i,), torus.other())

    sems, gain_sems = (send_sem, recv_sem), (gsend_sem, grecv_sem)

    def phase_one(c):
        first, mid, last = axes_of[c]
        return Direct(torus, first, sems, (c, 0), lambda i: bufs[c].at[pos[last], pos[mid], i])

    def phase_two(c):
        first, mid, last = axes_of[c]
        return Direct(torus, mid, sems, (c, 1), lambda i: bufs[c].at[pos[last], i])

    def phase_three(c, delta):
        first, mid, last = axes_of[c]
        return Gather(torus, last, sems, (c, 2 + delta), lambda i: bufs[c].at[i, torus.at(mid, delta)])

    def gain_places(buf):
        return (lambda i: buf.at[pos["z"], pos["y"], i], lambda i: buf.at[pos["z"], i], lambda i: buf.at[i])

    one = [phase_one(c) for c in colours]
    two = [phase_two(c) for c in colours]
    three = [[phase_three(c, d) for d in range(4)] for c in colours]
    gains = [Direct(torus, "xyz"[k], gain_sems, (k,), gain_places(gg)[k]) for k in range(3)]

    def each(items, step):
        for item in items:
            getattr(item, step)()

    each(one, "start")
    gains[0].start()

    @pl.when(first_core)
    def _():
        load_inputs.wait()
        turn(nat, x_t, 0, 8)
        for c in colours:
            one[c].finish()
            two[c].start()
            three[c][OWN].start()
        gains[0].finish()
        gains[1].start()
        for block in (BEFORE, AFTER):
            for c in colours:
                two[c].take(block)
                three[c][block].start()
        gains[1].finish()
        gains[2].start()
        for c in colours:
            two[c].take(FAR)
            three[c][FAR].start()
        pl.semaphore_signal(go_sem, inc=1, device_id=torus.other(), device_id_type=MESH)
        for c in colours:
            three[c][OWN].forward()
        gains[2].finish()
        gain_columns()
        total = prepare(0, 16)
        for c in colours:
            three[c][BEFORE].forward()
            three[c][AFTER].forward()
        total = total + prepare(16, 16)
        for c in colours:
            three[c][FAR].forward()
        factors(total)
        masks()

    @pl.when(second_core)
    def _():
        load_upstream.wait()
        each(one, "finish")
        each(two, "start")
        gains[0].finish()
        gains[1].start()
        turn(nat, c_t, 0, 8)
        gains[1].finish()
        gains[2].start()
        each(two, "finish")
        gains[2].finish()
        pl.semaphore_wait(go_sem, 1)
        for d in range(4):
            for c in colours:
                three[c][d].start()
        gain_columns()
        masks()
        for d in range(4):
            for c in colours:
                three[c][d].forward()
        total = jnp.zeros((8, 256), jnp.float32)
        for i in range(4):
            pass_on(i).wait_recv()
            total = total + prepare(8 * i, 8)
        factors(total)

    for c in colours:
        each(three[c], "finish")
        project(c)
    kv_t[...] = kv[...].T
    attention_forward()

    @pl.when(first_core)
    def _():
        for h in range(4):
            mix(2 * h)
            mix(2 * h + 1)
            pass_on(h).start()

    for trip in one + two + gains + three[0] + three[1] + three[2]:
        trip.sent()
    attention_backward()

    out_sems, out_gain_sems = (ssend_sem, srecv_sem), (sgsend_sem, sgrecv_sem)
    inboxes = ((r00, r01, r02), (r10, r11, r12), (r20, r21, r22))

    def last_phase(c, delta):
        first, mid, last = axes_of[c]
        return Scatter(
            torus, last, out_sems, (c, 2 + delta), lambda i: sums[c].at[i, torus.at(mid, delta)],
            inboxes[2][c].at[delta])

    def mid_phase(c):
        first, mid, last = axes_of[c]
        return Direct(torus, mid, out_sems, (c, 1), lambda i: sums[c].at[pos[last], i], inboxes[1][c])

    def first_phase(c):
        first, mid, last = axes_of[c]
        return Direct(torus, first, out_sems, (c, 0), lambda i: sums[c].at[pos[last], pos[mid], i], inboxes[0][c])

    home_three = [[last_phase(c, d) for d in range(4)] for c in colours]
    home_two = [mid_phase(c) for c in colours]
    home_one = [first_phase(c) for c in colours]
    home_gains = [
        Direct(torus, "xyz"[k], out_gain_sems, (k,), gain_places(bg)[k], (q0, q1, q2)[k]) for k in range(3)]

    def send_group(d):
        for c in colours:
            weight_grads(c, d)
            home_three[c][d].start()

    send_group(FAR)
    send_group(BEFORE)

    @pl.when(first_core)
    def _():
        send_group(AFTER)
        send_group(OWN)
        for i in range(4):
            pass_on(i).wait_send()

    through()
    for i in range(4):
        flow(8 * i, 8)
        pl.when(second_core)(pass_back(i).start)

    @pl.when(second_core)
    def _():
        send_group(AFTER)
        send_group(OWN)

    for c in colours:
        home_three[c][FAR].forward()
        home_three[c][BEFORE].forward()
    gain_grads()
    home_gains[2].start()
    turn_back()
    store = pltpu.make_async_copy(nat, out_ref, local_sem.at[7])
    store.start()
    for c in colours:
        home_three[c][AFTER].forward()
        home_three[c][FAR].finish()
        home_two[c].send(FAR)
    home_gains[2].finish()
    home_gains[1].start()
    for c in colours:
        home_three[c][OWN].forward()
        home_three[c][BEFORE].finish()
        home_two[c].send(BEFORE)
    home_gains[1].finish()
    home_gains[0].start()
    for c in colours:
        home_three[c][AFTER].finish()
        home_two[c].send(AFTER)
    for c in colours:
        home_three[c][OWN].finish()
    for c in colours:
        home_two[c].finish()
        home_one[c].start()
    home_gains[0].finish()
    each(home_one, "finish")

    def mine(c):
        return own_place(sums, c)[...].astype(jnp.float32)

    m1 = mine(1)
    key_out[:, 0:384] = mine(0)
    key_out[:, 384:512] = m1[:, 0:128]
    value_out[:, 0:256] = m1[:, 128:384]
    value_out[:, 256:512] = mine(2)
    slab = bg[pos["z"], pos["y"], pos["x"]][0:1]
    gain_out[...] = jnp.where(odd, slab[:, 64:128], slab[:, 0:64])

    for trip in home_one + home_two + home_gains + home_three[0] + home_three[1] + home_three[2]:
        trip.sent()
    store.wait()

    @pl.when(second_core)
    def _():
        for i in range(4):
            pass_back(i).wait_send()


def results_kernel(*refs):
    count = (len(refs) - 1) // 2
    sem = refs[-1]
    copies = []
    for src, dst in zip(refs[:count], refs[count:2 * count]):
        if src.shape[0] == 256:
            copies += [(src.at[pl.ds(32 * i, 32)], dst.at[pl.ds(32 * i, 32)]) for i in range(8)]
        else:
            copies.append((src, dst))
    copies = [pltpu.make_async_copy(src, dst, sem.at[i]) for i, (src, dst) in enumerate(copies)]
    for copy in copies:
        copy.start()
    for copy in copies:
        copy.wait()


def results(arrays):
    anywhere = pl.BlockSpec(memory_space=pl.ANY)
    return pl.pallas_call(
        results_kernel,
        out_shape=[jax.ShapeDtypeStruct(a.shape, a.dtype) for a in arrays],
        in_specs=[anywhere] * len(arrays),
        out_specs=[anywhere] * len(arrays),
        scratch_shapes=[pltpu.SemaphoreType.DMA((16,))],
        name="results",
    )(*arrays)


def layers(docs, gain, key_weight, value_weight, inputs, upstream):
    vmem = pl.BlockSpec(memory_space=pltpu.VMEM)
    anywhere = pl.BlockSpec(memory_space=pl.ANY)
    bf16, f32 = jnp.bfloat16, jnp.float32
    dma = pltpu.SemaphoreType.DMA
    slabs = [pltpu.VMEM((4, 4, 4, ROWS, w), bf16) for _, _, w in COLOURS] + [pltpu.VMEM((4, 4, 4, 8, 128), f32)]
    return pl.pallas_call(
        layer_kernel,
        out_shape=[
            jax.ShapeDtypeStruct((256, 4096), bf16),
            jax.ShapeDtypeStruct((ROWS, 512), f32),
            jax.ShapeDtypeStruct((ROWS, 512), f32),
            jax.ShapeDtypeStruct((1, ROWS), f32),
        ],
        in_specs=[pl.BlockSpec(memory_space=pltpu.SMEM), vmem, anywhere, anywhere, anywhere, anywhere],
        out_specs=[anywhere, vmem, vmem, vmem],
        scratch_shapes=slabs + slabs
        + [pltpu.VMEM((4, 6, 2, ROWS, w), bf16) for _, _, w in COLOURS]
        + [pltpu.VMEM((4, 4, ROWS, w), bf16) for _, _, w in COLOURS]
        + [pltpu.VMEM((4, ROWS, w), bf16) for _, _, w in COLOURS]
        + [pltpu.VMEM((4, 4, 4, 8, 128), f32), pltpu.VMEM((4, 4, 8, 128), f32), pltpu.VMEM((4, 8, 128), f32)]
        + [
            pltpu.VMEM((256, 4096), bf16),
            pltpu.VMEM((4096, 256), bf16),
            pltpu.VMEM((4096, 256), bf16),
            pltpu.VMEM((4096, 256), bf16),
            pltpu.VMEM((256, 4096), bf16),
            pltpu.VMEM((4096, 256), bf16),
            pltpu.VMEM((4096, 256), bf16),
            pltpu.VMEM((8, 128, 1024), bf16),
            pltpu.VMEM((256, 1024), bf16),
            pltpu.VMEM((1024, 256), bf16),
            pltpu.VMEM((256, 1024), bf16),
            pltpu.VMEM((256, 1024), bf16),
            pltpu.VMEM((1024, 256), bf16),
            pltpu.VMEM((4096, 128), bf16),
            pltpu.VMEM((2, 128, 128), f32),
            pltpu.VMEM((16, 256), f32),
        ]
        + [
            dma((8,)),
            dma((3, 6, 6)), dma((3, 6, 6)), dma((3, 4)), dma((3, 4)),
            dma((3, 6, 6)), dma((3, 6, 6)), dma((3, 4)), dma((3, 4)),
            dma((8,)), dma((8,)),
            pltpu.SemaphoreType.REGULAR,
        ],
        compiler_params=pltpu.CompilerParams(
            collective_id=0, has_side_effects=True, vmem_limit_bytes=58 * 1024 * 1024),
        name="layers",
    )(docs, gain, key_weight, value_weight, inputs, upstream)


def shards(inputs, upstream, doc_blocks, gain, key_weight, value_weight):
    flow, key_share, value_share, gain_share = results(layers(
        doc_blocks, gain, key_weight[0], value_weight[0], inputs.reshape(256, 4096), upstream.reshape(256, 4096)))
    return (flow.reshape(1, 2, 128, 4096), key_share[None], value_share[None], gain_share)


def solution(mesh):
    in_specs = (
        P("dp", None, None),
        P("dp", None, None),
        P("dp", None),
        P("section", "dp"),
        P("section", "dp", None),
        P("section", "dp", None),
    )
    out_specs = (
        P("section", "dp", None, None),
        P("section", "dp", None),
        P("section", "dp", None),
        P("section", "dp"),
    )
    return jax.shard_map(shards, mesh=mesh, in_specs=in_specs, out_specs=out_specs, check_vma=False)
```

```python
import jax
import jax.numpy as jnp
from jax import lax
from jax.experimental import pallas as pl
from jax.experimental.pallas import tpu as pltpu
from jax.sharding import PartitionSpec as P

HEAD_DIM = 128
BLOCK = 64
ROWS = 64
STRIDE = {"x": 1, "y": 4, "z": 16}
COLOURS = ((("x", "y", "z"), 0, 384), (("z", "y", "x"), 384, 384), (("x", "z", "y"), 768, 256))
OWN, AFTER, FAR, BEFORE = 0, 1, 2, 3
MESH = pl.DeviceIdType.MESH


class Torus:
    def __init__(self):
        self.section = lax.axis_index("section")
        self.me = lax.axis_index("dp")
        self.pos = {"x": lax.rem(self.me, 4), "y": lax.rem(self.me // 4, 4), "z": self.me // 16}

    def at(self, axis, delta):
        return lax.rem(self.pos[axis] + delta, 4)

    def peer(self, axis, delta):
        return (self.section, self.me + (self.at(axis, delta) - self.pos[axis]) * STRIDE[axis])

    def other(self):
        return (1 - self.section, self.me)

    def barrier(self):
        sem = pltpu.get_barrier_semaphore()
        for axis in "xyz":
            for delta in (1, 2, 3):
                pl.semaphore_signal(sem, inc=1, device_id=self.peer(axis, delta), device_id_type=MESH)
        pl.semaphore_signal(sem, inc=1, device_id=self.other(), device_id_type=MESH)
        pl.semaphore_wait(sem, 10)


def remote(src, dst, sems, index, device):
    return pltpu.make_async_remote_copy(
        src_ref=src, dst_ref=dst, send_sem=sems[0].at[index], recv_sem=sems[1].at[index],
        device_id=device, device_id_type=MESH)


def half(ref, which):
    size = ref.shape[0] // 2
    return ref.at[pl.ds(which * size, size)]


def add_into(dst, *others):
    for i in range(dst.shape[0]) if len(dst.shape) > 2 else (Ellipsis,):
        total = dst[i].astype(jnp.float32)
        for other in others:
            total = total + other[i].astype(jnp.float32)
        dst[i] = total.astype(dst.dtype)


class Ring:
    def __init__(self, torus, axis, sems, index, ref_at, inbox=None):
        self.torus, self.axis, self.sems, self.index, self.inbox = torus, axis, sems, index, inbox
        self.blocks = [ref_at(torus.at(axis, d)) for d in range(4)]

    def copy(self, k, src, dst, delta):
        return remote(src, dst, self.sems, self.index + (k,), self.torus.peer(self.axis, delta))

    def arrived(self, k, ref):
        self.copy(k, ref, ref, 1).wait_recv()


class Gather(Ring):
    def send(self, k, block, which, delta):
        ref = half(self.blocks[block], which)
        self.copy(k, ref, ref, delta).start()

    def start(self):
        self.send(0, OWN, 0, 1)
        self.send(2, OWN, 1, 3)
        self.send(1, OWN, 1, 1)
        self.send(3, OWN, 0, 3)

    def forward(self):
        self.arrived(0, half(self.blocks[BEFORE], 0))
        self.send(4, BEFORE, 0, 1)
        self.arrived(2, half(self.blocks[AFTER], 1))
        self.send(5, AFTER, 1, 3)

    def near(self):
        self.arrived(1, half(self.blocks[BEFORE], 1))
        self.arrived(3, half(self.blocks[AFTER], 0))

    def far(self):
        self.arrived(4, half(self.blocks[FAR], 0))
        self.arrived(5, half(self.blocks[FAR], 1))

    def finish(self):
        self.near()
        self.far()

    def sent(self):
        ref = half(self.blocks[OWN], 0)
        for k in range(6):
            self.copy(k, ref, ref, 1).wait_send()


class Scatter(Ring):
    def send(self, k, block, which, delta):
        self.copy(k, half(self.blocks[block], which), self.inbox.at[k], delta).start()

    def into(self, block, which, *slots):
        for k in slots:
            self.arrived(k, self.inbox.at[k])
        add_into(half(self.blocks[block], which), *[self.inbox.at[k] for k in slots])

    def start_far(self):
        self.send(0, FAR, 0, 1)
        self.send(1, FAR, 1, 3)

    def start_after(self):
        self.send(2, AFTER, 1, 1)

    def start_before(self):
        self.send(3, BEFORE, 0, 3)

    def start(self):
        self.start_far()
        self.start_after()
        self.start_before()

    def forward(self):
        self.into(AFTER, 0, 0)
        self.send(4, AFTER, 0, 1)
        self.into(BEFORE, 1, 1)
        self.send(5, BEFORE, 1, 3)

    def finish(self):
        self.into(OWN, 0, 3, 4)
        self.into(OWN, 1, 2, 5)

    def sent(self):
        for k in range(6):
            self.copy(k, self.inbox.at[k], self.inbox.at[k], 1).wait_send()


class Direct(Ring):
    def send(self, delta):
        if self.inbox is None:
            self.copy(delta, self.blocks[OWN], self.blocks[OWN], delta).start()
        else:
            self.copy(delta, self.blocks[delta], self.inbox.at[delta], delta).start()

    def start(self):
        for delta in (FAR, AFTER, BEFORE):
            self.send(delta)

    def take(self, block):
        self.arrived(4 - block, self.blocks[block])

    def finish(self):
        if self.inbox is None:
            for block in (AFTER, BEFORE, FAR):
                self.take(block)
        else:
            for k in (1, 3, 2):
                self.arrived(k, self.inbox.at[k])
            add_into(self.blocks[OWN], *[self.inbox.at[k] for k in (1, 2, 3)])

    def sent(self):
        for k in (1, 2, 3):
            self.copy(k, self.blocks[OWN], self.blocks[OWN], 1).wait_send()


def chunk_of(bufs, c, z, y):
    index = {"z": z, "y": y, "x": slice(None)}
    first, mid, last = COLOURS[c][0]
    return bufs[c].at[index[last], index[mid], index[first]]


def dot(a, b):
    return jnp.dot(a, b, preferred_element_type=jnp.float32)


def dot_nt(a, b):
    return lax.dot_general(a, b, (((1,), (1,)), ((), ())), preferred_element_type=jnp.float32)


def rows(i, size):
    if isinstance(i, int):
        return pl.ds(i * size, size)
    return pl.ds(pl.multiple_of(i * size, size), size)


def layer_kernel(
    docs_ref, gain_ref, key_ref, value_ref, inputs_ref, upstream_ref,
    out_ref, key_out, value_out, gain_out,
    g0, g1, g2, gg, b0, b1, b2, bg, r20, r21, r22, r10, r11, r12, r00, r01, r02, q2, q1, q0,
    nat, x_t, out_t, m_t, m_nat, c_t, dh_t, p_t, kv_sum, kv, kv_t, dkv, dkv_r, dkv_t, gcol, bias, stat,
    local_sem, send_sem, recv_sem, gsend_sem, grecv_sem, ssend_sem, srecv_sem, sgsend_sem, sgrecv_sem, cross_send, cross_recv,
    go_sem,
):
    torus = Torus()
    section, pos = torus.section, torus.pos
    bufs, sums = (g0, g1, g2), (b0, b1, b2)
    first_core, second_core = section == 0, section == 1
    odd = lax.rem(torus.me, 2) == 1
    colours = range(3)
    axes_of = [axes for axes, _, _ in COLOURS]

    def own_place(bufs, c):
        first, mid, last = axes_of[c]
        return bufs[c].at[pos[last], pos[mid], pos[first]]

    local = [
        pltpu.make_async_copy(key_ref.at[:, pl.ds(0, 384)], own_place(bufs, 0), local_sem.at[0]),
        pltpu.make_async_copy(key_ref.at[:, pl.ds(384, 128)], own_place(bufs, 1).at[:, pl.ds(0, 128)], local_sem.at[1]),
        pltpu.make_async_copy(value_ref.at[:, pl.ds(0, 256)], own_place(bufs, 1).at[:, pl.ds(128, 256)], local_sem.at[2]),
        pltpu.make_async_copy(value_ref.at[:, pl.ds(256, 256)], own_place(bufs, 2), local_sem.at[3]),
    ]
    for copy in local:
        copy.start()
    load_inputs = pltpu.make_async_copy(inputs_ref, nat, local_sem.at[5])
    load_upstream = pltpu.make_async_copy(upstream_ref, nat, local_sem.at[6])
    pl.when(first_core)(load_inputs.start)
    pl.when(second_core)(load_upstream.start)
    gain_row = gain_ref[...].astype(jnp.float32)
    still = jnp.zeros_like(gain_row)
    placed = jnp.where(odd, jnp.concatenate([still, gain_row], axis=1), jnp.concatenate([gain_row, still], axis=1))
    gg[pos["z"], pos["y"], pos["x"]] = jnp.broadcast_to(placed, (8, 128))
    torus.barrier()
    for copy in local:
        copy.wait()


    def turn(src, dst, start, count):
        for i in range(start, start + count):
            part = slice(512 * i, 512 * i + 512)
            dst[part, :] = src[:, part].T

    def gain_columns():
        for j in range(32):
            i = 2 * j
            row = gg[i // 16, i // 4 % 4, i % 4] + gg[i // 16, i // 4 % 4, i % 4 + 1]
            gcol[128 * j:128 * j + 128, :] = jnp.broadcast_to(row[0:1], (128, 128)).T.astype(jnp.bfloat16)

    def gains_of(part):
        once = gcol[part, :].astype(jnp.float32)
        return jnp.concatenate([once, once], axis=1)

    def prepare(start, count):
        total = jnp.zeros((8, 256), jnp.float32)
        for i in range(start, start + count):
            part = slice(128 * i, 128 * i + 128)
            x = x_t[part, :].astype(jnp.float32)
            m = (x * gains_of(part)).astype(jnp.bfloat16)
            m_t[part, :] = m
            m_nat[:, part] = m.T
            total = total + jnp.sum((x * x).reshape(16, 8, 256), axis=0)
        return total

    def factors(total):
        mean = jnp.sum(total, axis=0, keepdims=True) * (1.0 / 4096.0)
        stat[0:8] = jnp.broadcast_to(lax.rsqrt(mean + 1e-05), (8, 256))

    def factor_column():
        return stat[0:8].T[:, 0:1]

    def group_places(c, delta):
        mid = torus.at(axes_of[c][1], delta)
        return [(n, mid) if axes_of[c][1] == "y" else (mid, n) for n in range(4)]

    def project(c, places, begin):
        _, start, w = COLOURS[c]
        weight = jnp.concatenate([chunk_of(bufs, c, z, y)[...].reshape(256, w) for z, y in places], axis=0)
        hidden = jnp.concatenate([m_nat[:, rows(z * 4 + y, 256)] for z, y in places], axis=1)
        part = dot(hidden, weight)
        kv_sum[:, start:start + w] = part if begin else kv_sum[:, start:start + w] + part

    def projected():
        kv[...] = (kv_sum[...] * factor_column()).astype(jnp.bfloat16)
        kv_t[...] = kv[...].T

    def masks():
        key = lax.broadcasted_iota(jnp.int32, (128, 128), 0)
        query = lax.broadcasted_iota(jnp.int32, (128, 128), 1)
        same_block = (key >= BLOCK) == (query >= BLOCK)
        for b in range(2):
            together = jnp.broadcast_to(docs_ref[b, 0] == docs_ref[b, 1], (128, 128))
            allowed = (key <= query) & (same_block | together)
            bias[b] = jnp.where(allowed, 0.0, -1e30)

    scale = HEAD_DIM ** -0.5

    def heads(ref, h, b):
        return jnp.concatenate([ref[rows(h * 8 + j, 128), rows(b, 128)] for j in range(8)], axis=1)

    def token_row(row, b):
        return jnp.concatenate([stat[row:row + 1, rows(b, 128)]] * 8, axis=1)

    def attention_forward():
        for i in range(8):
            h, b = i // 2, i % 2
            scores = dot(kv[rows(b, 128), rows(h, 128)], heads(m_t, h, b))
            weights = jnp.exp(scores * (token_row(0, b) * scale) + jnp.concatenate([bias[b]] * 8, axis=1))
            share = 1.0 / jnp.sum(weights, axis=0, keepdims=True)
            p_t[i] = (weights * share).astype(jnp.bfloat16)

    def mix(i):
        h, b = i // 2, i % 2
        mixed = dot(kv_t[512 + 128 * h:640 + 128 * h, 128 * b:128 * b + 128], p_t[i])
        for j in range(8):
            at = (pl.ds((8 * h + j) * 128, 128), pl.ds(b * 128, 128))
            out_t[at] = (x_t[at].astype(jnp.float32) + mixed[:, 128 * j:128 * j + 128]).astype(jnp.bfloat16)

    def attention_backward():
        for i in range(8):
            h, b = i // 2, i % 2
            if b == 0:
                pl.when(first_core)(pass_back(h).wait_recv)
            c = heads(c_t, h, b)
            p = p_t[i]
            d_p = dot(kv[rows(b, 128), rows(4 + h, 128)], c)
            p_wide = p.astype(jnp.float32)
            inner = jnp.sum(p_wide * d_p, axis=0, keepdims=True)
            d_s = p_wide * (d_p - inner) * scale
            dkv[rows(b, 128), rows(4 + h, 128)] = dot_nt(p, c).astype(jnp.bfloat16)
            d_s_r = (d_s * token_row(0, b)).astype(jnp.bfloat16)
            dkv[rows(b, 128), rows(h, 128)] = dot_nt(d_s_r, heads(m_t, h, b)).astype(jnp.bfloat16)
            d_q = dot(kv_t[rows(h, 128), rows(b, 128)], d_s.astype(jnp.bfloat16))
            for j in range(8):
                dh_t[rows(h * 8 + j, 128), rows(b, 128)] = d_q[:, 128 * j:128 * j + 128].astype(jnp.bfloat16)
        dkv_t[...] = dkv[...].T
        dkv_r[...] = (dkv[...].astype(jnp.float32) * factor_column()).astype(jnp.bfloat16)

    def weight_grads(c, delta):
        _, start, w = COLOURS[c]
        for z, y in group_places(c, delta):
            part = dot(m_t[rows(z * 4 + y, 256), :], dkv_r[:, start:start + w]).astype(jnp.bfloat16)
            chunk_of(sums, c, z, y)[...] = part.reshape(4, ROWS, w)

    def through():
        factor = stat[0:1]
        dots = jnp.zeros((8, 256), jnp.float32)
        for i in range(16):
            z, y = i // 4, i % 4
            part = slice(256 * i, 256 * i + 256)
            weight = jnp.concatenate(
                [chunk_of(bufs, c, z, y)[...].reshape(256, w) for c, (_, _, w) in enumerate(COLOURS)], axis=1)
            d_h = (dh_t[part, :].astype(jnp.float32) + dot(weight, dkv_t[...])).astype(jnp.bfloat16)
            dh_t[part, :] = d_h
            both = d_h.astype(jnp.float32) * x_t[part, :].astype(jnp.float32)
            dots = dots + jnp.sum((both * gains_of(part)).reshape(32, 8, 256), axis=0)
        stat[8:9] = factor * factor * factor * jnp.sum(dots, axis=0, keepdims=True) * (1.0 / 4096.0)

    def gain_grads():
        lane = lax.broadcasted_iota(jnp.int32, (128, 128), 1)
        total = jnp.zeros((128, 128), jnp.float32)
        for j in range(32):
            part = slice(128 * j, 128 * j + 128)
            each = dh_t[part, :].astype(jnp.float32) * x_t[part, :].astype(jnp.float32) * stat[0:1]
            total = jnp.where(lane == j, jnp.sum(each, axis=1, keepdims=True), total)
        total = total.T
        for j in range(32):
            i = 2 * j
            row = jnp.broadcast_to(total[j:j + 1, :], (8, 128))
            bg[i // 16, i // 4 % 4, i % 4] = row
            bg[i // 16, i // 4 % 4, i % 4 + 1] = row

    def flow(start, count):
        for i in range(start, start + count):
            part = slice(128 * i, 128 * i + 128)
            u = dh_t[part, :].astype(jnp.float32) * gains_of(part)
            x = x_t[part, :].astype(jnp.float32)
            d_norm = (u * stat[0:1] - x * stat[8:9]).astype(jnp.bfloat16)
            out_t[part, :] = (c_t[part, :].astype(jnp.float32) + d_norm.astype(jnp.float32)).astype(jnp.bfloat16)

    def turn_back():
        for i in range(8):
            part = slice(512 * i, 512 * i + 512)
            nat[:, part] = out_t[part, :].T

    def pass_on(i):
        part = pl.ds(i * 1024, 1024)
        return remote(out_t.at[part], x_t.at[part], (cross_send, cross_recv), (i,), torus.other())

    def pass_back(i):
        part = pl.ds(i * 1024, 1024)
        return remote(out_t.at[part], c_t.at[part], (cross_send, cross_recv), (4 + i,), torus.other())

    sems, gain_sems = (send_sem, recv_sem), (gsend_sem, grecv_sem)

    def phase_one(c):
        first, mid, last = axes_of[c]
        return Direct(torus, first, sems, (c, 0), lambda i: bufs[c].at[pos[last], pos[mid], i])

    def phase_two(c):
        first, mid, last = axes_of[c]
        return Gather(torus, mid, sems, (c, 1), lambda i: bufs[c].at[pos[last], i])

    def phase_three(c, delta):
        first, mid, last = axes_of[c]
        return Gather(torus, last, sems, (c, 2 + delta), lambda i: bufs[c].at[i, torus.at(mid, delta)])

    def gain_places(buf):
        return (lambda i: buf.at[pos["z"], pos["y"], i], lambda i: buf.at[pos["z"], i], lambda i: buf.at[i])

    one = [phase_one(c) for c in colours]
    two = [phase_two(c) for c in colours]
    three = [[phase_three(c, d) for d in range(4)] for c in colours]
    gains = [Direct(torus, "xyz"[k], gain_sems, (k,), gain_places(gg)[k]) for k in range(3)]

    def each(items, step):
        for item in items:
            getattr(item, step)()

    each(one, "start")
    gains[0].start()

    def gather_middle(turned):
        for c in colours:
            one[c].finish()
            two[c].start()
            three[c][OWN].start()
        gains[0].finish()
        gains[1].start()
        turn(nat, turned, 0, 8)
        for c in colours:
            two[c].forward()

    def gather_gains():
        gains[1].finish()
        gains[2].start()
        for c in colours:
            three[c][OWN].forward()

    def arrive():
        for d in (OWN, BEFORE, AFTER, FAR):
            for c in colours:
                three[c][d].finish()
            for c in colours:
                project(c, group_places(c, d), d == OWN)

    @pl.when(first_core)
    def _():
        load_inputs.wait()
        gather_middle(x_t)
        for c in colours:
            two[c].near()
            three[c][BEFORE].start()
            three[c][AFTER].start()
        gather_gains()
        for c in colours:
            two[c].far()
            three[c][FAR].start()
        gains[2].finish()
        gain_columns()
        total = prepare(0, 16)
        for c in colours:
            three[c][BEFORE].forward()
            three[c][AFTER].forward()
        total = total + prepare(16, 16)
        for c in colours:
            three[c][FAR].forward()
        pl.semaphore_signal(go_sem, inc=1, device_id=torus.other(), device_id_type=MESH)
        factors(total)
        masks()
        arrive()

    @pl.when(second_core)
    def _():
        load_upstream.wait()
        gather_middle(c_t)
        gather_gains()
        each(two, "finish")
        gains[2].finish()
        pl.semaphore_wait(go_sem, 1)
        for d in (BEFORE, AFTER, FAR):
            for c in colours:
                three[c][d].start()
        gain_columns()
        masks()
        for d in (BEFORE, AFTER, FAR):
            for c in colours:
                three[c][d].forward()
        total = jnp.zeros((8, 256), jnp.float32)
        for i in range(4):
            pass_on(i).wait_recv()
            total = total + prepare(8 * i, 8)
        factors(total)
        arrive()

    projected()
    attention_forward()

    @pl.when(first_core)
    def _():
        for h in range(4):
            mix(2 * h)
            mix(2 * h + 1)
            pass_on(h).start()

    for trip in one + two + gains + three[0] + three[1] + three[2]:
        trip.sent()
    attention_backward()

    out_sems, out_gain_sems = (ssend_sem, srecv_sem), (sgsend_sem, sgrecv_sem)
    inboxes = ((r00, r01, r02), (r10, r11, r12), (r20, r21, r22))

    def last_phase(c, delta):
        first, mid, last = axes_of[c]
        return Scatter(
            torus, last, out_sems, (c, 2 + delta), lambda i: sums[c].at[i, torus.at(mid, delta)],
            inboxes[2][c].at[delta])

    def mid_phase(c):
        first, mid, last = axes_of[c]
        return Scatter(torus, mid, out_sems, (c, 1), lambda i: sums[c].at[pos[last], i], inboxes[1][c])

    def first_phase(c):
        first, mid, last = axes_of[c]
        return Direct(torus, first, out_sems, (c, 0), lambda i: sums[c].at[pos[last], pos[mid], i], inboxes[0][c])

    home_three = [[last_phase(c, d) for d in range(4)] for c in colours]
    home_two = [mid_phase(c) for c in colours]
    home_one = [first_phase(c) for c in colours]
    home_gains = [
        Direct(torus, "xyz"[k], out_gain_sems, (k,), gain_places(bg)[k], (q0, q1, q2)[k]) for k in range(3)]

    def send_group(d):
        for c in colours:
            weight_grads(c, d)
            home_three[c][d].start()

    send_group(FAR)
    send_group(BEFORE)

    @pl.when(first_core)
    def _():
        send_group(AFTER)
        send_group(OWN)
        for i in range(4):
            pass_on(i).wait_send()

    through()
    for i in range(4):
        flow(8 * i, 8)
        pl.when(second_core)(pass_back(i).start)

    @pl.when(second_core)
    def _():
        send_group(AFTER)
        send_group(OWN)

    gain_grads()
    home_gains[2].start()
    for d in (FAR, BEFORE, AFTER, OWN):
        for c in colours:
            home_three[c][d].forward()
    turn_back()
    store = pltpu.make_async_copy(nat, out_ref, local_sem.at[7])
    store.start()
    home_gains[2].finish()
    home_gains[1].start()
    for c in colours:
        home_three[c][FAR].finish()
        home_two[c].start_far()
    for c in colours:
        home_three[c][BEFORE].finish()
        home_two[c].start_before()
    for c in colours:
        home_three[c][AFTER].finish()
        home_two[c].start_after()
    home_gains[1].finish()
    home_gains[0].start()
    each(home_two, "forward")
    for c in colours:
        home_three[c][OWN].finish()
    for c in colours:
        home_two[c].finish()
        home_one[c].start()
    home_gains[0].finish()
    each(home_one, "finish")

    def mine(c):
        return own_place(sums, c)[...].astype(jnp.float32)

    m1 = mine(1)
    key_out[:, 0:384] = mine(0)
    key_out[:, 384:512] = m1[:, 0:128]
    value_out[:, 0:256] = m1[:, 128:384]
    value_out[:, 256:512] = mine(2)
    slab = bg[pos["z"], pos["y"], pos["x"]][0:1]
    gain_out[...] = jnp.where(odd, slab[:, 64:128], slab[:, 0:64])

    for trip in home_one + home_two + home_gains + home_three[0] + home_three[1] + home_three[2]:
        trip.sent()
    store.wait()

    @pl.when(second_core)
    def _():
        for i in range(4):
            pass_back(i).wait_send()


def results_kernel(*refs):
    count = len(refs) // 2
    for src, dst in zip(refs[:count], refs[count:]):
        dst[...] = src[...]


def results(arrays):
    def spec(a):
        if a.shape[0] == 1:
            return pl.BlockSpec(a.shape, lambda i: (0, 0))
        return pl.BlockSpec((a.shape[0] // 2, a.shape[1]), lambda i: (i, 0))

    return pl.pallas_call(
        results_kernel,
        grid=(2,),
        out_shape=[jax.ShapeDtypeStruct(a.shape, a.dtype) for a in arrays],
        in_specs=[spec(a) for a in arrays],
        out_specs=[spec(a) for a in arrays],
        name="results",
    )(*arrays)


def layers(docs, gain, key_weight, value_weight, inputs, upstream):
    vmem = pl.BlockSpec(memory_space=pltpu.VMEM)
    anywhere = pl.BlockSpec(memory_space=pl.ANY)
    bf16, f32 = jnp.bfloat16, jnp.float32
    dma = pltpu.SemaphoreType.DMA
    slabs = [pltpu.VMEM((4, 4, 4, ROWS, w), bf16) for _, _, w in COLOURS] + [pltpu.VMEM((4, 4, 4, 8, 128), f32)]
    return pl.pallas_call(
        layer_kernel,
        out_shape=[
            jax.ShapeDtypeStruct((256, 4096), bf16),
            jax.ShapeDtypeStruct((ROWS, 512), f32),
            jax.ShapeDtypeStruct((ROWS, 512), f32),
            jax.ShapeDtypeStruct((1, ROWS), f32),
        ],
        in_specs=[pl.BlockSpec(memory_space=pltpu.SMEM), vmem, anywhere, anywhere, anywhere, anywhere],
        out_specs=[anywhere, vmem, vmem, vmem],
        scratch_shapes=slabs + slabs
        + [pltpu.VMEM((4, 6, 2, ROWS, w), bf16) for _, _, w in COLOURS]
        + [pltpu.VMEM((6, 2, ROWS, w), bf16) for _, _, w in COLOURS]
        + [pltpu.VMEM((4, ROWS, w), bf16) for _, _, w in COLOURS]
        + [pltpu.VMEM((4, 4, 4, 8, 128), f32), pltpu.VMEM((4, 4, 8, 128), f32), pltpu.VMEM((4, 8, 128), f32)]
        + [
            pltpu.VMEM((256, 4096), bf16),
            pltpu.VMEM((4096, 256), bf16),
            pltpu.VMEM((4096, 256), bf16),
            pltpu.VMEM((4096, 256), bf16),
            pltpu.VMEM((256, 4096), bf16),
            pltpu.VMEM((4096, 256), bf16),
            pltpu.VMEM((4096, 256), bf16),
            pltpu.VMEM((8, 128, 1024), bf16),
            pltpu.VMEM((256, 1024), f32),
            pltpu.VMEM((256, 1024), bf16),
            pltpu.VMEM((1024, 256), bf16),
            pltpu.VMEM((256, 1024), bf16),
            pltpu.VMEM((256, 1024), bf16),
            pltpu.VMEM((1024, 256), bf16),
            pltpu.VMEM((4096, 128), bf16),
            pltpu.VMEM((2, 128, 128), f32),
            pltpu.VMEM((16, 256), f32),
        ]
        + [
            dma((8,)),
            dma((3, 6, 6)), dma((3, 6, 6)), dma((3, 4)), dma((3, 4)),
            dma((3, 6, 6)), dma((3, 6, 6)), dma((3, 4)), dma((3, 4)),
            dma((8,)), dma((8,)),
            pltpu.SemaphoreType.REGULAR,
        ],
        compiler_params=pltpu.CompilerParams(
            collective_id=0, has_side_effects=True, vmem_limit_bytes=58 * 1024 * 1024),
        name="layers",
    )(docs, gain, key_weight, value_weight, inputs, upstream)


def shards(inputs, upstream, doc_blocks, gain, key_weight, value_weight):
    flow, key_share, value_share, gain_share = results(layers(
        doc_blocks, gain, key_weight[0], value_weight[0], inputs.reshape(256, 4096), upstream.reshape(256, 4096)))
    return (flow.reshape(1, 2, 128, 4096), key_share[None], value_share[None], gain_share)


def solution(mesh):
    in_specs = (
        P("dp", None, None),
        P("dp", None, None),
        P("dp", None),
        P("section", "dp"),
        P("section", "dp", None),
        P("section", "dp", None),
    )
    out_specs = (
        P("section", "dp", None, None),
        P("section", "dp", None),
        P("section", "dp", None),
        P("section", "dp"),
    )
    return jax.shard_map(shards, mesh=mesh, in_specs=in_specs, out_specs=out_specs, check_vma=False)
```

```python
import jax
import jax.numpy as jnp
from jax import lax
from jax.experimental import pallas as pl
from jax.experimental.pallas import tpu as pltpu
from jax.sharding import PartitionSpec as P

HEAD_DIM = 128
BLOCK = 64
ROWS = 64
STRIDE = {"x": 1, "y": 4, "z": 16}
COLOURS = ((("x", "y", "z"), 0, 384), (("z", "y", "x"), 384, 384), (("x", "z", "y"), 768, 256))
OWN, AFTER, FAR, BEFORE = 0, 1, 2, 3
MESH = pl.DeviceIdType.MESH


class Torus:
    def __init__(self):
        self.section = lax.axis_index("section")
        self.me = lax.axis_index("dp")
        self.pos = {"x": lax.rem(self.me, 4), "y": lax.rem(self.me // 4, 4), "z": self.me // 16}

    def at(self, axis, delta):
        return lax.rem(self.pos[axis] + delta, 4)

    def peer(self, axis, delta):
        return (self.section, self.me + (self.at(axis, delta) - self.pos[axis]) * STRIDE[axis])

    def other(self):
        return (1 - self.section, self.me)

    def greet(self):
        sem = pltpu.get_barrier_semaphore()
        for axis in "xyz":
            for delta in (1, 2, 3):
                pl.semaphore_signal(sem, inc=1, device_id=self.peer(axis, delta), device_id_type=MESH)
        pl.semaphore_signal(sem, inc=1, device_id=self.other(), device_id_type=MESH)

    def all_here(self):
        pl.semaphore_wait(pltpu.get_barrier_semaphore(), 10)


def remote(src, dst, sems, index, device):
    return pltpu.make_async_remote_copy(
        src_ref=src, dst_ref=dst, send_sem=sems[0].at[index], recv_sem=sems[1].at[index],
        device_id=device, device_id_type=MESH)


def half(ref, which):
    size = ref.shape[0] // 2
    return ref.at[pl.ds(which * size, size)]


def add_into(dst, *others):
    for i in range(dst.shape[0]) if len(dst.shape) > 2 else (Ellipsis,):
        total = dst[i].astype(jnp.float32)
        for other in others:
            total = total + other[i].astype(jnp.float32)
        dst[i] = total.astype(dst.dtype)


class Ring:
    def __init__(self, torus, axis, sems, index, ref_at, inbox=None):
        self.torus, self.axis, self.sems, self.index, self.inbox = torus, axis, sems, index, inbox
        self.blocks = [ref_at(torus.at(axis, d)) for d in range(4)]

    def copy(self, k, src, dst, delta):
        return remote(src, dst, self.sems, self.index + (k,), self.torus.peer(self.axis, delta))

    def arrived(self, k, ref):
        self.copy(k, ref, ref, 1).wait_recv()


class Gather(Ring):
    def send(self, k, block, which, delta):
        ref = half(self.blocks[block], which)
        self.copy(k, ref, ref, delta).start()

    def start(self):
        self.send(0, OWN, 0, 1)
        self.send(2, OWN, 1, 3)
        self.send(1, OWN, 1, 1)
        self.send(3, OWN, 0, 3)

    def forward(self):
        self.arrived(0, half(self.blocks[BEFORE], 0))
        self.send(4, BEFORE, 0, 1)
        self.arrived(2, half(self.blocks[AFTER], 1))
        self.send(5, AFTER, 1, 3)

    def near(self):
        self.arrived(1, half(self.blocks[BEFORE], 1))
        self.arrived(3, half(self.blocks[AFTER], 0))

    def far(self):
        self.arrived(4, half(self.blocks[FAR], 0))
        self.arrived(5, half(self.blocks[FAR], 1))

    def finish(self):
        self.near()
        self.far()

    def sent(self):
        ref = half(self.blocks[OWN], 0)
        for k in range(6):
            self.copy(k, ref, ref, 1).wait_send()


class Scatter(Ring):
    def send(self, k, block, which, delta):
        self.copy(k, half(self.blocks[block], which), self.inbox.at[k], delta).start()

    def into(self, block, which, *slots):
        for k in slots:
            self.arrived(k, self.inbox.at[k])
        add_into(half(self.blocks[block], which), *[self.inbox.at[k] for k in slots])

    def start_far(self):
        self.send(0, FAR, 0, 1)
        self.send(1, FAR, 1, 3)

    def start_after(self):
        self.send(2, AFTER, 1, 1)

    def start_before(self):
        self.send(3, BEFORE, 0, 3)

    def start(self):
        self.start_far()
        self.start_after()
        self.start_before()

    def forward(self):
        self.into(AFTER, 0, 0)
        self.send(4, AFTER, 0, 1)
        self.into(BEFORE, 1, 1)
        self.send(5, BEFORE, 1, 3)

    def finish(self):
        self.into(OWN, 0, 3, 4)
        self.into(OWN, 1, 2, 5)

    def sent(self):
        for k in range(6):
            self.copy(k, self.inbox.at[k], self.inbox.at[k], 1).wait_send()


class Direct(Ring):
    def send(self, delta):
        if self.inbox is None:
            self.copy(delta, self.blocks[OWN], self.blocks[OWN], delta).start()
        else:
            self.copy(delta, self.blocks[delta], self.inbox.at[delta], delta).start()

    def start(self):
        for delta in (FAR, AFTER, BEFORE):
            self.send(delta)

    def take(self, block):
        self.arrived(4 - block, self.blocks[block])

    def finish(self):
        if self.inbox is None:
            for block in (AFTER, BEFORE, FAR):
                self.take(block)
        else:
            for k in (1, 3, 2):
                self.arrived(k, self.inbox.at[k])
            add_into(self.blocks[OWN], *[self.inbox.at[k] for k in (1, 2, 3)])

    def sent(self):
        for k in (1, 2, 3):
            self.copy(k, self.blocks[OWN], self.blocks[OWN], 1).wait_send()


def chunk_of(bufs, c, z, y):
    index = {"z": z, "y": y, "x": slice(None)}
    first, mid, last = COLOURS[c][0]
    return bufs[c].at[index[last], index[mid], index[first]]


def dot(a, b):
    return jnp.dot(a, b, preferred_element_type=jnp.float32)


def dot_nt(a, b):
    return lax.dot_general(a, b, (((1,), (1,)), ((), ())), preferred_element_type=jnp.float32)


def rows(i, size):
    if isinstance(i, int):
        return pl.ds(i * size, size)
    return pl.ds(pl.multiple_of(i * size, size), size)


def layer_kernel(
    docs_ref, gain_ref, key_ref, value_ref, inputs_ref, upstream_ref,
    out_ref, key_out, value_out, gain_out,
    g0, g1, g2, gg, b0, b1, b2, bg, r20, r21, r22, r10, r11, r12, r00, r01, r02, q2, q1, q0,
    nat, x_t, out_t, m_t, m_nat, c_t, dh_t, p_t, kv_sum, kv, kv_t, dkv, dkv_r, dkv_t, gcol, bias, stat,
    local_sem, send_sem, recv_sem, gsend_sem, grecv_sem, ssend_sem, srecv_sem, sgsend_sem, sgrecv_sem, cross_send, cross_recv,
    go_sem,
):
    torus = Torus()
    torus.greet()
    section, pos = torus.section, torus.pos
    bufs, sums = (g0, g1, g2), (b0, b1, b2)
    first_core, second_core = section == 0, section == 1
    odd = lax.rem(torus.me, 2) == 1
    colours = range(3)
    axes_of = [axes for axes, _, _ in COLOURS]

    def own_place(bufs, c):
        first, mid, last = axes_of[c]
        return bufs[c].at[pos[last], pos[mid], pos[first]]

    local = [
        pltpu.make_async_copy(key_ref.at[:, pl.ds(0, 384)], own_place(bufs, 0), local_sem.at[0]),
        pltpu.make_async_copy(key_ref.at[:, pl.ds(384, 128)], own_place(bufs, 1).at[:, pl.ds(0, 128)], local_sem.at[1]),
        pltpu.make_async_copy(value_ref.at[:, pl.ds(0, 256)], own_place(bufs, 1).at[:, pl.ds(128, 256)], local_sem.at[2]),
        pltpu.make_async_copy(value_ref.at[:, pl.ds(256, 256)], own_place(bufs, 2), local_sem.at[3]),
    ]
    for copy in local:
        copy.start()
    load_inputs = pltpu.make_async_copy(inputs_ref, nat, local_sem.at[5])
    load_upstream = pltpu.make_async_copy(upstream_ref, nat, local_sem.at[6])
    pl.when(first_core)(load_inputs.start)
    pl.when(second_core)(load_upstream.start)
    gain_row = gain_ref[...].astype(jnp.float32)
    still = jnp.zeros_like(gain_row)
    placed = jnp.where(odd, jnp.concatenate([still, gain_row], axis=1), jnp.concatenate([gain_row, still], axis=1))
    gg[pos["z"], pos["y"], pos["x"]] = jnp.broadcast_to(placed, (8, 128))
    torus.all_here()
    for copy in local:
        copy.wait()


    def turn(src, dst, start, count):
        for i in range(start, start + count):
            part = slice(512 * i, 512 * i + 512)
            dst[part, :] = src[:, part].T

    def gain_columns():
        for j in range(32):
            i = 2 * j
            row = gg[i // 16, i // 4 % 4, i % 4] + gg[i // 16, i // 4 % 4, i % 4 + 1]
            gcol[128 * j:128 * j + 128, :] = jnp.broadcast_to(row[0:1], (128, 128)).T.astype(jnp.bfloat16)

    def gains_of(part):
        once = gcol[part, :].astype(jnp.float32)
        return jnp.concatenate([once, once], axis=1)

    def prepare(start, count):
        total = jnp.zeros((8, 256), jnp.float32)
        for i in range(start, start + count):
            part = slice(128 * i, 128 * i + 128)
            x = x_t[part, :].astype(jnp.float32)
            m = (x * gains_of(part)).astype(jnp.bfloat16)
            m_t[part, :] = m
            m_nat[:, part] = m.T
            total = total + jnp.sum((x * x).reshape(16, 8, 256), axis=0)
        return total

    def factors(total):
        mean = jnp.sum(total, axis=0, keepdims=True) * (1.0 / 4096.0)
        stat[0:8] = jnp.broadcast_to(lax.rsqrt(mean + 1e-05), (8, 256))

    def factor_column():
        return stat[0:8].T[:, 0:1]

    def group_places(c, delta):
        mid = torus.at(axes_of[c][1], delta)
        return [(n, mid) if axes_of[c][1] == "y" else (mid, n) for n in range(4)]

    def project(c, places, begin):
        _, start, w = COLOURS[c]
        weight = jnp.concatenate([chunk_of(bufs, c, z, y)[...].reshape(256, w) for z, y in places], axis=0)
        hidden = jnp.concatenate([m_nat[:, rows(z * 4 + y, 256)] for z, y in places], axis=1)
        part = dot(hidden, weight)
        kv_sum[:, start:start + w] = part if begin else kv_sum[:, start:start + w] + part

    def projected():
        kv[...] = (kv_sum[...] * factor_column()).astype(jnp.bfloat16)
        kv_t[...] = kv[...].T

    def masks():
        key = lax.broadcasted_iota(jnp.int32, (128, 128), 0)
        query = lax.broadcasted_iota(jnp.int32, (128, 128), 1)
        same_block = (key >= BLOCK) == (query >= BLOCK)
        for b in range(2):
            together = jnp.broadcast_to(docs_ref[b, 0] == docs_ref[b, 1], (128, 128))
            allowed = (key <= query) & (same_block | together)
            bias[b] = jnp.where(allowed, 0.0, -1e30)

    scale = HEAD_DIM ** -0.5

    def heads(ref, h, b):
        return jnp.concatenate([ref[rows(h * 8 + j, 128), rows(b, 128)] for j in range(8)], axis=1)

    def token_row(row, b):
        return jnp.concatenate([stat[row:row + 1, rows(b, 128)]] * 8, axis=1)

    def attention_forward():
        for i in range(8):
            h, b = i // 2, i % 2
            scores = dot(kv[rows(b, 128), rows(h, 128)], heads(m_t, h, b))
            weights = jnp.exp(scores * (token_row(0, b) * scale) + jnp.concatenate([bias[b]] * 8, axis=1))
            share = 1.0 / jnp.sum(weights, axis=0, keepdims=True)
            p_t[i] = (weights * share).astype(jnp.bfloat16)

    def mix(i):
        h, b = i // 2, i % 2
        mixed = dot(kv_t[512 + 128 * h:640 + 128 * h, 128 * b:128 * b + 128], p_t[i])
        for j in range(8):
            at = (pl.ds((8 * h + j) * 128, 128), pl.ds(b * 128, 128))
            out_t[at] = (x_t[at].astype(jnp.float32) + mixed[:, 128 * j:128 * j + 128]).astype(jnp.bfloat16)

    def attention_backward():
        for i in range(8):
            h, b = i // 2, i % 2
            if b == 0:
                pl.when(first_core)(pass_back(h).wait_recv)
            c = heads(c_t, h, b)
            p = p_t[i]
            d_p = dot(kv[rows(b, 128), rows(4 + h, 128)], c)
            p_wide = p.astype(jnp.float32)
            inner = jnp.sum(p_wide * d_p, axis=0, keepdims=True)
            d_s = p_wide * (d_p - inner) * scale
            dkv[rows(b, 128), rows(4 + h, 128)] = dot_nt(p, c).astype(jnp.bfloat16)
            d_s_r = (d_s * token_row(0, b)).astype(jnp.bfloat16)
            dkv[rows(b, 128), rows(h, 128)] = dot_nt(d_s_r, heads(m_t, h, b)).astype(jnp.bfloat16)
            d_q = dot(kv_t[rows(h, 128), rows(b, 128)], d_s.astype(jnp.bfloat16))
            for j in range(8):
                dh_t[rows(h * 8 + j, 128), rows(b, 128)] = d_q[:, 128 * j:128 * j + 128].astype(jnp.bfloat16)
        dkv_t[...] = dkv[...].T
        dkv_r[...] = (dkv[...].astype(jnp.float32) * factor_column()).astype(jnp.bfloat16)

    def weight_grads(c, delta):
        _, start, w = COLOURS[c]
        for z, y in group_places(c, delta):
            part = dot(m_t[rows(z * 4 + y, 256), :], dkv_r[:, start:start + w]).astype(jnp.bfloat16)
            chunk_of(sums, c, z, y)[...] = part.reshape(4, ROWS, w)

    def through():
        factor = stat[0:1]
        dots = jnp.zeros((8, 256), jnp.float32)
        for i in range(16):
            z, y = i // 4, i % 4
            part = slice(256 * i, 256 * i + 256)
            weight = jnp.concatenate(
                [chunk_of(bufs, c, z, y)[...].reshape(256, w) for c, (_, _, w) in enumerate(COLOURS)], axis=1)
            d_h = (dh_t[part, :].astype(jnp.float32) + dot(weight, dkv_t[...])).astype(jnp.bfloat16)
            dh_t[part, :] = d_h
            both = d_h.astype(jnp.float32) * x_t[part, :].astype(jnp.float32)
            dots = dots + jnp.sum((both * gains_of(part)).reshape(32, 8, 256), axis=0)
        stat[8:9] = factor * factor * factor * jnp.sum(dots, axis=0, keepdims=True) * (1.0 / 4096.0)

    def gain_grads():
        lane = lax.broadcasted_iota(jnp.int32, (128, 128), 1)
        total = jnp.zeros((128, 128), jnp.float32)
        for j in range(32):
            part = slice(128 * j, 128 * j + 128)
            each = dh_t[part, :].astype(jnp.float32) * x_t[part, :].astype(jnp.float32) * stat[0:1]
            total = jnp.where(lane == j, jnp.sum(each, axis=1, keepdims=True), total)
        total = total.T
        for j in range(32):
            i = 2 * j
            row = jnp.broadcast_to(total[j:j + 1, :], (8, 128))
            bg[i // 16, i // 4 % 4, i % 4] = row
            bg[i // 16, i // 4 % 4, i % 4 + 1] = row

    def flow(start, count):
        for i in range(start, start + count):
            part = slice(128 * i, 128 * i + 128)
            u = dh_t[part, :].astype(jnp.float32) * gains_of(part)
            x = x_t[part, :].astype(jnp.float32)
            d_norm = (u * stat[0:1] - x * stat[8:9]).astype(jnp.bfloat16)
            out_t[part, :] = (c_t[part, :].astype(jnp.float32) + d_norm.astype(jnp.float32)).astype(jnp.bfloat16)

    def turn_back():
        for i in range(8):
            part = slice(512 * i, 512 * i + 512)
            nat[:, part] = out_t[part, :].T

    def pass_on(i):
        part = pl.ds(i * 1024, 1024)
        return remote(out_t.at[part], x_t.at[part], (cross_send, cross_recv), (i,), torus.other())

    def pass_back(i):
        part = pl.ds(i * 1024, 1024)
        return remote(out_t.at[part], c_t.at[part], (cross_send, cross_recv), (4 + i,), torus.other())

    sems, gain_sems = (send_sem, recv_sem), (gsend_sem, grecv_sem)

    def phase_one(c):
        first, mid, last = axes_of[c]
        return Direct(torus, first, sems, (c, 0), lambda i: bufs[c].at[pos[last], pos[mid], i])

    def phase_two(c):
        first, mid, last = axes_of[c]
        return Gather(torus, mid, sems, (c, 1), lambda i: bufs[c].at[pos[last], i])

    def phase_three(c, delta):
        first, mid, last = axes_of[c]
        return Gather(torus, last, sems, (c, 2 + delta), lambda i: bufs[c].at[i, torus.at(mid, delta)])

    def gain_places(buf):
        return (lambda i: buf.at[pos["z"], pos["y"], i], lambda i: buf.at[pos["z"], i], lambda i: buf.at[i])

    one = [phase_one(c) for c in colours]
    two = [phase_two(c) for c in colours]
    three = [[phase_three(c, d) for d in range(4)] for c in colours]
    gains = [Direct(torus, "xyz"[k], gain_sems, (k,), gain_places(gg)[k]) for k in range(3)]

    def each(items, step):
        for item in items:
            getattr(item, step)()

    each(one, "start")
    gains[0].start()

    def gather_middle(turned):
        for c in colours:
            one[c].finish()
            two[c].start()
            three[c][OWN].start()
        gains[0].finish()
        gains[1].start()
        turn(nat, turned, 0, 8)
        for c in colours:
            two[c].forward()

    def gather_gains():
        gains[1].finish()
        gains[2].start()
        for c in colours:
            three[c][OWN].forward()

    def arrive():
        for d in (OWN, BEFORE, AFTER, FAR):
            for c in colours:
                three[c][d].finish()
            for c in colours:
                project(c, group_places(c, d), d == OWN)

    @pl.when(first_core)
    def _():
        load_inputs.wait()
        gather_middle(x_t)
        for c in colours:
            two[c].near()
            three[c][BEFORE].start()
            three[c][AFTER].start()
        gather_gains()
        for c in colours:
            two[c].far()
            three[c][FAR].start()
        gains[2].finish()
        gain_columns()
        total = prepare(0, 16)
        for c in colours:
            three[c][BEFORE].forward()
            three[c][AFTER].forward()
        total = total + prepare(16, 16)
        for c in colours:
            three[c][FAR].forward()
        pl.semaphore_signal(go_sem, inc=1, device_id=torus.other(), device_id_type=MESH)
        factors(total)
        masks()
        arrive()

    @pl.when(second_core)
    def _():
        load_upstream.wait()
        gather_middle(c_t)
        gather_gains()
        each(two, "finish")
        gains[2].finish()
        pl.semaphore_wait(go_sem, 1)
        for d in (BEFORE, AFTER, FAR):
            for c in colours:
                three[c][d].start()
        gain_columns()
        masks()
        for d in (BEFORE, AFTER, FAR):
            for c in colours:
                three[c][d].forward()
        total = jnp.zeros((8, 256), jnp.float32)
        for i in range(4):
            pass_on(i).wait_recv()
            total = total + prepare(8 * i, 8)
        factors(total)
        arrive()

    projected()
    attention_forward()

    @pl.when(first_core)
    def _():
        for h in range(4):
            mix(2 * h)
            mix(2 * h + 1)
            pass_on(h).start()

    for trip in one + two + gains + three[0] + three[1] + three[2]:
        trip.sent()
    attention_backward()

    out_sems, out_gain_sems = (ssend_sem, srecv_sem), (sgsend_sem, sgrecv_sem)
    inboxes = ((r00, r01, r02), (r10, r11, r12), (r20, r21, r22))

    def last_phase(c, delta):
        first, mid, last = axes_of[c]
        return Scatter(
            torus, last, out_sems, (c, 2 + delta), lambda i: sums[c].at[i, torus.at(mid, delta)],
            inboxes[2][c].at[delta])

    def mid_phase(c):
        first, mid, last = axes_of[c]
        return Scatter(torus, mid, out_sems, (c, 1), lambda i: sums[c].at[pos[last], i], inboxes[1][c])

    def first_phase(c):
        first, mid, last = axes_of[c]
        return Direct(torus, first, out_sems, (c, 0), lambda i: sums[c].at[pos[last], pos[mid], i], inboxes[0][c])

    home_three = [[last_phase(c, d) for d in range(4)] for c in colours]
    home_two = [mid_phase(c) for c in colours]
    home_one = [first_phase(c) for c in colours]
    home_gains = [
        Direct(torus, "xyz"[k], out_gain_sems, (k,), gain_places(bg)[k], (q0, q1, q2)[k]) for k in range(3)]

    def send_group(d):
        for c in colours:
            weight_grads(c, d)
            home_three[c][d].start()

    for d in (FAR, BEFORE, AFTER, OWN):
        send_group(d)

    @pl.when(first_core)
    def _():
        for i in range(4):
            pass_on(i).wait_send()

    through()
    for i in range(4):
        flow(8 * i, 8)
        pl.when(second_core)(pass_back(i).start)

    gain_grads()
    home_gains[2].start()
    for d in (FAR, BEFORE, AFTER, OWN):
        for c in colours:
            home_three[c][d].forward()
    turn_back()
    store = pltpu.make_async_copy(nat, out_ref, local_sem.at[7])
    store.start()
    home_gains[2].finish()
    home_gains[1].start()
    for c in colours:
        home_three[c][FAR].finish()
        home_two[c].start_far()
    for c in colours:
        home_three[c][BEFORE].finish()
        home_two[c].start_before()
    for c in colours:
        home_three[c][AFTER].finish()
        home_two[c].start_after()
    home_gains[1].finish()
    home_gains[0].start()
    each(home_two, "forward")
    for c in colours:
        home_three[c][OWN].finish()
    for c in colours:
        home_two[c].finish()
        home_one[c].start()
    home_gains[0].finish()
    each(home_one, "finish")

    def mine(c):
        return own_place(sums, c)[...].astype(jnp.float32)

    m1 = mine(1)
    key_out[:, 0:384] = mine(0)
    key_out[:, 384:512] = m1[:, 0:128]
    value_out[:, 0:256] = m1[:, 128:384]
    value_out[:, 256:512] = mine(2)
    slab = bg[pos["z"], pos["y"], pos["x"]][0:1]
    gain_out[...] = jnp.where(odd, slab[:, 64:128], slab[:, 0:64])

    for trip in home_one + home_two + home_gains + home_three[0] + home_three[1] + home_three[2]:
        trip.sent()
    store.wait()

    @pl.when(second_core)
    def _():
        for i in range(4):
            pass_back(i).wait_send()


def results_kernel(*refs):
    count = len(refs) // 2
    for src, dst in zip(refs[:count], refs[count:]):
        dst[...] = src[...]


def results(arrays):
    def spec(a):
        if a.shape[0] == 1:
            return pl.BlockSpec(a.shape, lambda i: (0, 0))
        return pl.BlockSpec((a.shape[0] // 2, a.shape[1]), lambda i: (i, 0))

    return pl.pallas_call(
        results_kernel,
        grid=(2,),
        out_shape=[jax.ShapeDtypeStruct(a.shape, a.dtype) for a in arrays],
        in_specs=[spec(a) for a in arrays],
        out_specs=[spec(a) for a in arrays],
        name="results",
    )(*arrays)


def layers(docs, gain, key_weight, value_weight, inputs, upstream):
    vmem = pl.BlockSpec(memory_space=pltpu.VMEM)
    anywhere = pl.BlockSpec(memory_space=pl.ANY)
    bf16, f32 = jnp.bfloat16, jnp.float32
    dma = pltpu.SemaphoreType.DMA
    slabs = [pltpu.VMEM((4, 4, 4, ROWS, w), bf16) for _, _, w in COLOURS] + [pltpu.VMEM((4, 4, 4, 8, 128), f32)]
    return pl.pallas_call(
        layer_kernel,
        out_shape=[
            jax.ShapeDtypeStruct((256, 4096), bf16),
            jax.ShapeDtypeStruct((ROWS, 512), f32),
            jax.ShapeDtypeStruct((ROWS, 512), f32),
            jax.ShapeDtypeStruct((1, ROWS), f32),
        ],
        in_specs=[pl.BlockSpec(memory_space=pltpu.SMEM), vmem, anywhere, anywhere, anywhere, anywhere],
        out_specs=[anywhere, vmem, vmem, vmem],
        scratch_shapes=slabs + slabs
        + [pltpu.VMEM((4, 6, 2, ROWS, w), bf16) for _, _, w in COLOURS]
        + [pltpu.VMEM((6, 2, ROWS, w), bf16) for _, _, w in COLOURS]
        + [pltpu.VMEM((4, ROWS, w), bf16) for _, _, w in COLOURS]
        + [pltpu.VMEM((4, 4, 4, 8, 128), f32), pltpu.VMEM((4, 4, 8, 128), f32), pltpu.VMEM((4, 8, 128), f32)]
        + [
            pltpu.VMEM((256, 4096), bf16),
            pltpu.VMEM((4096, 256), bf16),
            pltpu.VMEM((4096, 256), bf16),
            pltpu.VMEM((4096, 256), bf16),
            pltpu.VMEM((256, 4096), bf16),
            pltpu.VMEM((4096, 256), bf16),
            pltpu.VMEM((4096, 256), bf16),
            pltpu.VMEM((8, 128, 1024), bf16),
            pltpu.VMEM((256, 1024), f32),
            pltpu.VMEM((256, 1024), bf16),
            pltpu.VMEM((1024, 256), bf16),
            pltpu.VMEM((256, 1024), bf16),
            pltpu.VMEM((256, 1024), bf16),
            pltpu.VMEM((1024, 256), bf16),
            pltpu.VMEM((4096, 128), bf16),
            pltpu.VMEM((2, 128, 128), f32),
            pltpu.VMEM((16, 256), f32),
        ]
        + [
            dma((8,)),
            dma((3, 6, 6)), dma((3, 6, 6)), dma((3, 4)), dma((3, 4)),
            dma((3, 6, 6)), dma((3, 6, 6)), dma((3, 4)), dma((3, 4)),
            dma((8,)), dma((8,)),
            pltpu.SemaphoreType.REGULAR,
        ],
        compiler_params=pltpu.CompilerParams(
            collective_id=0, has_side_effects=True, vmem_limit_bytes=58 * 1024 * 1024),
        name="layers",
    )(docs, gain, key_weight, value_weight, inputs, upstream)


def shards(inputs, upstream, doc_blocks, gain, key_weight, value_weight):
    flow, key_share, value_share, gain_share = results(layers(
        doc_blocks, gain, key_weight[0], value_weight[0], inputs.reshape(256, 4096), upstream.reshape(256, 4096)))
    return (flow.reshape(1, 2, 128, 4096), key_share[None], value_share[None], gain_share)


def solution(mesh):
    in_specs = (
        P("dp", None, None),
        P("dp", None, None),
        P("dp", None),
        P("section", "dp"),
        P("section", "dp", None),
        P("section", "dp", None),
    )
    out_specs = (
        P("section", "dp", None, None),
        P("section", "dp", None),
        P("section", "dp", None),
        P("section", "dp"),
    )
    return jax.shard_map(shards, mesh=mesh, in_specs=in_specs, out_specs=out_specs, check_vma=False)
```
